128 devices in a mesh: row: 8 (over x, core), col: 16 (over y, z).
Axes of the slice: x: 4, y: 4, z: 4, core: 2. Of those that a mesh axis runs over, the one named last changes fastest.
Arguments:
- panel: float32 [8192, 512], P(('row', 'col')), as said below
- trailing: float32 [8192, 32768], P('row', 'col'), may hold values from -6 to 6
Outputs:
- r_factor: float32 [512, 512], replicated
- coupling: float32 [512, 32768], P(None, 'col')
- trailing_out: float32 [8192, 32768], P('row', 'col')
The draws below stay inside these ranges and needn't reach their ends.
Inputs may be any that keep to these rules, and one draw needn't show every extreme that they name: The panel has full column rank with moderate conditioning; its rows carry scales that differ, and its columns share a common component.
All inputs are finite; a program needn't handle non-finite values.
Results may differ from the reference program's by a relative error of at most 0.000086.
Values sent between devices are 32-bit elements; how exact they have to be, the bound alone decides.
No kernel may reach another device: no remote copies, remote signals or barrier semaphores. Data moves between devices by JAX's collectives and lax.ppermute only.
A program may use at most 128 MiB of HBM per device.

```python
import math
import jax
import jax.numpy as jnp
from jax import lax

B = 512
ROWS = 8192
TRAIL = 32768


def draw_panel(key, part):
    key = jax.random.fold_in(key, 11)
    first, second, third = jax.random.split(key, 3)
    base = jax.random.normal(first, (ROWS, B), jnp.float32)
    common = jax.random.normal(second, (ROWS, 8), jnp.float32)
    scales = jnp.exp(jax.random.uniform(third, (ROWS,), jnp.float32, 0.0, math.log(10.0)))
    mixed = base + 0.75 * jnp.tile(common, (1, B // 8))
    return (mixed * scales[:, None] * (0.25 / math.sqrt(ROWS))).astype(jnp.float32)


def block_scale(rng, extent, pieces, smallest, largest):
    gain, own = 1.0, jax.random.fold_in(rng, 6)
    for axis_at, parts in pieces:
        heights = jnp.exp(jax.random.uniform(jax.random.fold_in(own, axis_at), (parts,), jnp.float32, smallest / len(pieces), largest / len(pieces)))
        gain = gain * jnp.repeat(heights, extent[axis_at] // parts).reshape([-1 if axis == axis_at else 1 for axis in range(len(extent))])
    return gain


def centred(key, dims, scale, limit, pieces=(), dtype=jnp.bfloat16):
    drawn = scale * jax.random.normal(key, dims, jnp.float32)
    if pieces:
        drawn = drawn * block_scale(key, dims, pieces, -0.22, 0.18)
    return jnp.clip(drawn, -limit, limit).astype(dtype)


def setup_inputs(seed: int = 0) -> dict:
    arg_keys = jax.random.split(jax.random.key(seed), 3)
    panel = draw_panel(jax.random.fold_in(arg_keys[2], 71), 0)
    trailing = centred(arg_keys[1], (ROWS, TRAIL), 1.0, 6.0, ((0, 8), (1, 16)), jnp.float32)
    return dict(panel=panel, trailing=trailing)


def reference(panel, trailing):
    gram = jnp.dot(panel.T.astype(jnp.float32), panel.astype(jnp.float32), precision=lax.Precision.HIGHEST, preferred_element_type=jnp.float32)
    lower = jnp.linalg.cholesky(gram)
    r_factor = lower.T
    basis = lax.linalg.triangular_solve(lower, panel, left_side=False, lower=True, transpose_a=True)
    coupling = jnp.dot(basis.T.astype(jnp.float32), trailing.astype(jnp.float32), precision=lax.Precision.HIGHEST, preferred_element_type=jnp.float32)
    trailing_out = trailing - jnp.dot(basis.astype(jnp.float32), coupling.astype(jnp.float32), precision=lax.Precision.HIGHEST, preferred_element_type=jnp.float32)
    return (r_factor, coupling, trailing_out)
```

```python
import functools

import jax
import jax.numpy as jnp
from jax import lax
from jax.experimental import pallas as pl
from jax.experimental.pallas import tpu as pltpu
from jax.sharding import PartitionSpec as P

HIGHEST = lax.Precision.HIGHEST
HIGH = lax.Precision.HIGH
F32 = jnp.float32
GROUP = 32
CHUNKS = 2


def near(i):
    return i ^ 1


def far(i):
    return 3 - i


CORE = [(r, r ^ 1) for r in range(8)]
XPAIR = [[(x * 2 + c, pair(x) * 2 + c) for x in range(4) for c in range(2)] for pair in (near, far)]
YPAIR = [[(y * 4 + z, pair(y) * 4 + z) for y in range(4) for z in range(4)] for pair in (near, far)]
ZPAIR = [[(y * 4 + z, y * 4 + pair(z)) for y in range(4) for z in range(4)] for pair in (near, far)]


def ring_bits(i):
    return (i ^ (i // 2)) & 1, i // 2


def tdot(a, b, precision=HIGHEST):
    return lax.dot_general(a, b, (((0,), (0,)), ((), ())), precision=precision, preferred_element_type=F32)


def spread(v, s):
    return jnp.broadcast_to(v[s:s + 1, :], (8, 128))


def eliminate(slab, off, g):
    nt = g // 8
    width = slab.shape[1] // 128
    sub = lax.broadcasted_iota(jnp.int32, (8, 128), 0)
    rows = [[slab[8 * t:8 * t + 8, 128 * w:128 * w + 128] for w in range(width)] for t in range(nt)]
    cols = [
        [jnp.broadcast_to(rows[t][0][:, off + k:off + k + 1], (8, 128)) if t >= k // 8 else None for t in range(nt)]
        for k in range(g)
    ]
    scale = [None] * nt
    for j in range(g):
        tj, sj = divmod(j, 8)
        d = spread(cols[j][tj], sj)
        inv = 1.0 / d
        root = lax.rsqrt(d)
        scale[tj] = root if sj == 0 else jnp.where(sub >= sj, root, scale[tj])
        f = [None if t < tj else cols[j][t] * inv for t in range(nt)]
        for k in range(j + 1, g):
            a = spread(cols[j][k // 8], k % 8)
            for t in range(k // 8, nt):
                cols[k][t] = cols[k][t] - f[t] * a
        f[tj] = jnp.where(sub > sj, f[tj], 0.0)
        for w in range(width):
            p = spread(rows[tj][w], sj)
            for t in range(tj, nt):
                if t > tj or sj < 7:
                    rows[t][w] = rows[t][w] - f[t] * p
    return jnp.concatenate(
        [jnp.concatenate([rows[t][w] * scale[t] for w in range(width)], axis=1) for t in range(nt)], axis=0
    )


def factor_kernel(g_ref, r_ref, inv_ref, m, w):
    b = r_ref.shape[0]
    nb = b // 128
    at = 0
    for i in range(nb):
        for j in range(i, nb):
            m[i * 128:i * 128 + 128, j * 128:j * 128 + 128] = g_ref[at:at + 128, :]
            at += 128
    ri = lax.broadcasted_iota(jnp.int32, (b, b), 0)
    ci = lax.broadcasted_iota(jnp.int32, (b, b), 1)
    m[:, b:] = jnp.where(ri == ci, 1.0, 0.0)

    @pl.loop(0, nb)
    def _(k):
        r0 = pl.multiple_of(k * 128, 128)
        win = pl.ds(r0, b + 128)
        for q in range(128 // GROUP):
            lo, hi = q * GROUP, (q + 1) * GROUP
            slab = m[pl.ds(r0 + lo, GROUP), win]
            if q:
                slab = slab - tdot(w[0:lo, lo:hi], w[0:lo, :])
            w[lo:hi, :] = eliminate(slab, lo, GROUP)
        m[pl.ds(r0, 128), win] = w[...]

        @pl.loop(k + 1, nb)
        def _(i):
            rows = pl.ds(pl.multiple_of(i * 128, 128), 128)
            u = w[:, pl.ds(pl.multiple_of((i - k) * 128, 128), 128)]
            m[rows, win] = m[rows, win] - tdot(u, w[...])

    for i in range(nb):
        for j in range(nb):
            block = m[i * 128:i * 128 + 128, j * 128:j * 128 + 128]
            if j < i:
                block = jnp.zeros((128, 128), F32)
            elif j == i:
                block = jnp.where(ri[:128, :128] <= ci[:128, :128], block, 0.0)
            r_ref[i * 128:i * 128 + 128, j * 128:j * 128 + 128] = block
    inv_ref[...] = m[:, b:]


def factor(packed, b):
    square = jax.ShapeDtypeStruct((b, b), F32)
    return pl.pallas_call(
        factor_kernel,
        out_shape=(square, square),
        scratch_shapes=[pltpu.VMEM((b, 2 * b), F32), pltpu.VMEM((128, b + 128), F32)],
        compiler_params=pltpu.CompilerParams(vmem_limit_bytes=24 << 20),
        cost_estimate=pl.CostEstimate(flops=10 ** 9, bytes_accessed=60 * 10 ** 6, transcendentals=0),
        name="factor",
    )(packed)


def assemble_kernel(order_ref, a0, a1, a2, a3, o_ref):
    for q, ref in enumerate((a0, a1, a2, a3)):
        for p in range(16):
            at = pl.multiple_of(order_ref[q, p] * 64, 64)
            o_ref[pl.ds(at, 64), q * 128:q * 128 + 128] = ref[p * 64:p * 64 + 64, :]


def gather_panel(panel):
    col = lax.axis_index("col")
    y, z = col // 4, col % 4
    pairs = {"y": YPAIR, "z": ZPAIR}
    orders = (
        (("z", 0), ("z", 1), ("y", 0), ("y", 1)),
        (("z", 1), ("z", 0), ("y", 1), ("y", 0)),
        (("y", 0), ("y", 1), ("z", 0), ("z", 1)),
        (("y", 1), ("y", 0), ("z", 1), ("z", 0)),
    )
    held = [panel[:, q * 128:q * 128 + 128] for q in range(4)]
    where = [[(y, z)] for _ in range(4)]
    flip = (near, far)
    for step in range(4):
        got = []
        for q in range(4):
            axis, side = orders[q][step]
            got.append(lax.ppermute(held[q], "col", pairs[axis][side]))
        for q in range(4):
            axis, side = orders[q][step]
            held[q] = jnp.concatenate([held[q], got[q]], axis=0)
            other = [(flip[side](a), b) if axis == "y" else (a, flip[side](b)) for a, b in where[q]]
            where[q] = where[q] + other
    table = jnp.stack([jnp.stack([a * 4 + b for a, b in where[q]]) for q in range(4)]).astype(jnp.int32)
    return pl.pallas_call(
        assemble_kernel,
        out_shape=jax.ShapeDtypeStruct((1024, 512), F32),
        in_specs=[pl.BlockSpec(memory_space=pltpu.SMEM)] + [pl.BlockSpec(memory_space=pltpu.VMEM)] * 4,
        out_specs=pl.BlockSpec(memory_space=pltpu.VMEM),
        compiler_params=pltpu.CompilerParams(vmem_limit_bytes=24 << 20),
        name="assemble",
    )(table, *held)


def halves(a, bit):
    n = a.shape[0] // 2
    return lax.dynamic_slice_in_dim(a, bit * n, n), lax.dynamic_slice_in_dim(a, (1 - bit) * n, n)


def join(own, other, bit):
    first = bit == 0
    return jnp.concatenate([jnp.where(first, own, other), jnp.where(first, other, own)], axis=0)


def sum_packed(a):
    core = lax.axis_index("row") % 2
    keep, give = halves(a, core)
    a = keep + lax.ppermute(give, "row", CORE)
    n = a.shape[0] // 2
    one, two = a[:n], a[n:]
    for side in (0, 1):
        one, two = (
            one + lax.ppermute(one, "row", XPAIR[side]),
            two + lax.ppermute(two, "row", XPAIR[1 - side]),
        )
    a = jnp.concatenate([one, two], axis=0)
    return join(a, lax.ppermute(a, "row", CORE), core)


def sum_scattered(a):
    row = lax.axis_index("row")
    core = row % 2
    bits = ring_bits(row // 2)
    keep, give = halves(a, core)
    a = keep + lax.ppermute(give, "row", CORE)
    n = a.shape[0] // 2
    parts = [a[:n], a[n:]]
    for step in (0, 1):
        sides = (step, 1 - step)
        cut = [halves(p, bits[s]) for p, s in zip(parts, sides)]
        got = [lax.ppermute(c[1], "row", XPAIR[s]) for c, s in zip(cut, sides)]
        parts = [c[0] + g for c, g in zip(cut, got)]
    for step in (1, 0):
        sides = (step, 1 - step)
        got = [lax.ppermute(p, "row", XPAIR[s]) for p, s in zip(parts, sides)]
        parts = [join(p, g, bits[s]) for p, g, s in zip(parts, got, sides)]
    a = jnp.concatenate(parts, axis=0)
    return join(a, lax.ppermute(a, "row", CORE), core)


def product(a, b, precision=HIGH):
    return jnp.dot(a, b, precision=precision, preferred_element_type=F32)


def local(panel, trailing):
    b = panel.shape[1]
    rows = gather_panel(panel)
    blocks = []
    for i in range(b // 128):
        strip = tdot(rows[:, i * 128:i * 128 + 128], rows[:, i * 128:])
        blocks += [strip[:, j:j + 128] for j in range(0, strip.shape[1], 128)]
    packed = sum_packed(jnp.concatenate(blocks, axis=0))
    width = trailing.shape[1] // CHUNKS
    pieces = [trailing[:, c * width:c * width + width] for c in range(CHUNKS)]
    sums = [sum_scattered(tdot(rows, piece, HIGH)) for piece in pieces]
    r_factor, inverse = factor(packed, b)
    basis = lax.dot_general(rows, inverse, (((1,), (1,)), ((), ())), precision=HIGH, preferred_element_type=F32)
    coupling = [product(inverse, s) for s in sums]
    out = [piece - product(basis, c) for piece, c in zip(pieces, coupling)]
    return (r_factor, jnp.concatenate(coupling, axis=1), jnp.concatenate(out, axis=1))


def solution(mesh):
    placed = (P(("row", "col"), None), P("row", "col"))
    return jax.shard_map(
        local,
        mesh=mesh,
        in_specs=placed,
        out_specs=(P(), P(None, "col"), P("row", "col")),
        check_vma=False,
    )
```

```python
import functools

import jax
import jax.numpy as jnp
from jax import lax
from jax.experimental import pallas as pl
from jax.experimental.pallas import tpu as pltpu
from jax.sharding import PartitionSpec as P

HIGHEST = lax.Precision.HIGHEST
BF16 = jnp.bfloat16
F32 = jnp.float32
GROUP = 32
TILE = 512


def near(i):
    return i ^ 1


def far(i):
    return 3 - i


CORE = [(r, r ^ 1) for r in range(8)]
XPAIR = [[(x * 2 + c, pair(x) * 2 + c) for x in range(4) for c in range(2)] for pair in (near, far)]
YPAIR = [[(y * 4 + z, pair(y) * 4 + z) for y in range(4) for z in range(4)] for pair in (near, far)]
ZPAIR = [[(y * 4 + z, y * 4 + pair(z)) for y in range(4) for z in range(4)] for pair in (near, far)]


def ring_bits(i):
    return (i ^ (i // 2)) & 1, i // 2


def tdot(a, b, precision=HIGHEST):
    return lax.dot_general(a, b, (((0,), (0,)), ((), ())), precision=precision, preferred_element_type=F32)


def spread(v, s):
    return jnp.broadcast_to(v[s:s + 1, :], (8, 128))


def eliminate(slab, off, g):
    nt = g // 8
    width = slab.shape[1] // 128
    sub = lax.broadcasted_iota(jnp.int32, (8, 128), 0)
    rows = [[slab[8 * t:8 * t + 8, 128 * w:128 * w + 128] for w in range(width)] for t in range(nt)]
    cols = [
        [jnp.broadcast_to(rows[t][0][:, off + k:off + k + 1], (8, 128)) if t >= k // 8 else None for t in range(nt)]
        for k in range(g)
    ]
    scale = [None] * nt
    for j in range(g):
        tj, sj = divmod(j, 8)
        d = spread(cols[j][tj], sj)
        inv = 1.0 / d
        root = lax.rsqrt(d)
        scale[tj] = root if sj == 0 else jnp.where(sub >= sj, root, scale[tj])
        f = [None if t < tj else cols[j][t] * inv for t in range(nt)]
        for k in range(j + 1, g):
            a = spread(cols[j][k // 8], k % 8)
            for t in range(k // 8, nt):
                cols[k][t] = cols[k][t] - f[t] * a
        f[tj] = jnp.where(sub > sj, f[tj], 0.0)
        for w in range(width):
            p = spread(rows[tj][w], sj)
            for t in range(tj, nt):
                if t > tj or sj < 7:
                    rows[t][w] = rows[t][w] - f[t] * p
    return jnp.concatenate(
        [jnp.concatenate([rows[t][w] * scale[t] for w in range(width)], axis=1) for t in range(nt)], axis=0
    )


def params(mib=40):
    return pltpu.CompilerParams(vmem_limit_bytes=mib << 20)


def whole(n=1):
    return [pl.BlockSpec(memory_space=pltpu.VMEM)] * n


SCALARS = pl.BlockSpec(memory_space=pltpu.SMEM)


def split(a):
    high = a.astype(BF16)
    return high, (a - high.astype(F32)).astype(BF16)


def dot(a, b):
    return jnp.dot(a, b, preferred_element_type=F32)


def dot3(a, b):
    return dot(a[0], b[0]) + (dot(a[0], b[1]) + dot(a[1], b[0]))


def factor_kernel(k, nb, *refs):
    earlier, g_ref, w, m = refs[:k], refs[k], refs[k + 1], refs[k + 2]
    first = sum(nb - i for i in range(k)) * 128
    for j in range(nb - k):
        m[:, j * 128:j * 128 + 128] = g_ref[first + j * 128:first + j * 128 + 128, :]
    if k:
        m[:, (nb - k) * 128:nb * 128] = jnp.zeros((128, k * 128), F32)
    ri = lax.broadcasted_iota(jnp.int32, (128, 128), 0)
    ci = lax.broadcasted_iota(jnp.int32, (128, 128), 1)
    m[:, nb * 128:] = jnp.where(ri == ci, 1.0, 0.0)
    for i in range(k):
        at = (k - i) * 128
        known = earlier[i][:, at:]
        width = known.shape[1]
        m[:, :width] = m[:, :width] - tdot(earlier[i][:, at:at + 128], known)
    for q in range(128 // GROUP):
        lo, hi = q * GROUP, (q + 1) * GROUP
        slab = m[lo:hi, :]
        if q:
            slab = slab - tdot(w[0:lo, lo:hi], w[0:lo, :])
        w[lo:hi, :] = eliminate(slab, lo, GROUP)


def factor_rows(k, nb, earlier, packed):
    window = (nb + 1) * 128
    return pl.pallas_call(
        functools.partial(factor_kernel, k, nb),
        out_shape=jax.ShapeDtypeStruct((128, window), F32),
        in_specs=whole(k + 1),
        out_specs=whole()[0],
        scratch_shapes=[pltpu.VMEM((128, window), F32)],
        compiler_params=params(16),
        cost_estimate=pl.CostEstimate(flops=5 * 10 ** 9, bytes_accessed=18 * 10 ** 6, transcendentals=0),
        name="factor",
    )(*earlier, packed)


def gram_kernel(order_ref, a0, a1, a2, a3, o_ref, keep_ref, give_ref, blocks):
    for q, ref in enumerate((a0, a1, a2, a3)):
        for p in range(16):
            at = pl.multiple_of(order_ref[q * 16 + p] * 64, 64)
            o_ref[pl.ds(at, 64), q * 128:q * 128 + 128] = ref[p * 64:p * 64 + 64, :]
    at = 0
    for i in range(4):
        strip = tdot(o_ref[:, i * 128:i * 128 + 128], o_ref[:, i * 128:])
        for j in range(4 - i):
            blocks[at:at + 128, :] = strip[:, j * 128:j * 128 + 128]
            at += 128
    core = order_ref[64]
    keep_ref[...] = blocks[pl.ds(pl.multiple_of(core * 640, 128), 640), :]
    give_ref[...] = blocks[pl.ds(pl.multiple_of((1 - core) * 640, 128), 640), :]


def gather_panel(panel, core):
    col = lax.axis_index("col")
    y, z = col // 4, col % 4
    pairs = {"y": YPAIR, "z": ZPAIR}
    orders = (
        (("z", 0), ("z", 1), ("y", 0), ("y", 1)),
        (("z", 1), ("z", 0), ("y", 1), ("y", 0)),
        (("y", 0), ("y", 1), ("z", 0), ("z", 1)),
        (("y", 1), ("y", 0), ("z", 1), ("z", 0)),
    )
    held = [panel[:, q * 128:q * 128 + 128] for q in range(4)]
    where = [[(y, z)] for _ in range(4)]
    flip = (near, far)
    for step in range(4):
        got = []
        for q in range(4):
            axis, side = orders[q][step]
            got.append(lax.ppermute(held[q], "col", pairs[axis][side]))
        for q in range(4):
            axis, side = orders[q][step]
            held[q] = jnp.concatenate([held[q], got[q]], axis=0)
            other = [(flip[side](a), b) if axis == "y" else (a, flip[side](b)) for a, b in where[q]]
            where[q] = where[q] + other
    table = jnp.stack([a * 4 + b for q in range(4) for a, b in where[q]] + [core]).astype(jnp.int32)
    half = jax.ShapeDtypeStruct((640, 128), F32)
    return pl.pallas_call(
        gram_kernel,
        out_shape=(jax.ShapeDtypeStruct((1024, 512), F32), half, half),
        in_specs=[SCALARS] + whole(4),
        out_specs=whole(3),
        scratch_shapes=[pltpu.VMEM((1280, 128), F32)],
        compiler_params=params(),
        name="gram",
    )(table, *held)


def join(own, other, bit):
    first = bit == 0
    return jnp.concatenate([jnp.where(first, own, other), jnp.where(first, other, own)], axis=0)


def swap(a, pairs):
    return lax.ppermute(a, "row", pairs)


def sum_packed(keep, give, core):
    a = keep + swap(give, CORE)
    n = a.shape[0] // 2
    one, two = a[:n], a[n:]
    for side in (0, 1):
        one, two = one + swap(one, XPAIR[side]), two + swap(two, XPAIR[1 - side])
    a = jnp.concatenate([one, two], axis=0)
    return join(a, swap(a, CORE), core)


def turn_kernel(p_ref, hi_ref, lo_ref):
    for j in range(0, 1024, 128):
        hi_ref[:, j:j + 128], lo_ref[:, j:j + 128] = split(jnp.transpose(p_ref[j:j + 128, :]))


def turn(rows):
    out = jax.ShapeDtypeStruct((rows.shape[1], rows.shape[0]), BF16)
    return pl.pallas_call(
        turn_kernel, out_shape=(out, out), in_specs=whole(), out_specs=whole(2), compiler_params=params(), name="turn"
    )(rows)


def share_kernel(table_ref, hi_ref, lo_ref, t_ref, o_ref):
    rows = pl.ds(pl.multiple_of(table_ref[0] * 256, 256), 256)
    got = dot3((hi_ref[rows, :], lo_ref[rows, :]), split(t_ref[...]))
    for p in range(8):
        at = pl.multiple_of(table_ref[1 + p] * 32, 32)
        o_ref[pl.ds(at, 32), :] = got[p * 32:p * 32 + 32, :]


def share(table, hi, lo, trailing):
    depth, width = trailing.shape
    return pl.pallas_call(
        share_kernel,
        out_shape=jax.ShapeDtypeStruct((256, width), F32),
        grid=(width // TILE,),
        in_specs=[SCALARS] + whole(2) + [pl.BlockSpec((depth, TILE), lambda i: (0, i))],
        out_specs=pl.BlockSpec((256, TILE), lambda i: (0, i)),
        compiler_params=params(),
        cost_estimate=pl.CostEstimate(flops=3 * 10 ** 9, bytes_accessed=12 * 10 ** 6, transcendentals=0),
        name="share",
    )(table, hi, lo, trailing)


def prepare_kernel(w0, w1, w2, w3, p_ref, r_ref, ihi_ref, ilo_ref, bhi_ref, blo_ref, inv):
    ri = lax.broadcasted_iota(jnp.int32, (128, 128), 0)
    ci = lax.broadcasted_iota(jnp.int32, (128, 128), 1)
    zero = jnp.zeros((128, 128), F32)
    for i, w in enumerate((w0, w1, w2, w3)):
        rows = slice(i * 128, i * 128 + 128)
        for j in range(4):
            cols = slice(j * 128, j * 128 + 128)
            if j < i:
                r_ref[rows, cols] = zero
            else:
                block = w[:, (j - i) * 128:(j - i) * 128 + 128]
                r_ref[rows, cols] = jnp.where(ri <= ci, block, 0.0) if j == i else block
            inv[rows, cols] = w[:, (4 - i + j) * 128:(5 - i + j) * 128] if j <= i else zero
    ihi_ref[...], ilo_ref[...] = split(inv[...])
    turned = split(jnp.transpose(inv[...]))
    for at in range(0, 1024, 256):
        rows = slice(at, at + 256)
        bhi_ref[rows, :], blo_ref[rows, :] = split(dot3(split(p_ref[rows, :]), turned))


def prepare(factors, rows):
    b = rows.shape[1]
    square, tall = (b, b), rows.shape
    return pl.pallas_call(
        prepare_kernel,
        out_shape=[jax.ShapeDtypeStruct(s, t) for s, t in ((square, F32), (square, BF16), (square, BF16), (tall, BF16), (tall, BF16))],
        in_specs=whole(5),
        out_specs=whole(5),
        scratch_shapes=[pltpu.VMEM(square, F32)],
        compiler_params=params(),
        cost_estimate=pl.CostEstimate(flops=3 * 10 ** 9, bytes_accessed=10 * 10 ** 6, transcendentals=0),
        name="prepare",
    )(*factors, rows)


def finish_kernel(table_ref, *refs):
    pieces, (ihi, ilo, bhi, blo, t_ref, c_ref, o_ref, total) = refs[:8], refs[8:]
    for p in range(8):
        for half in (0, 1):
            at = pl.multiple_of(table_ref[2 * p + half] * 32, 32)
            total[pl.ds(at, 32), :] = pieces[p][half * 32:half * 32 + 32, :]
    coupling = dot3((ihi[...], ilo[...]), split(total[...]))
    c_ref[...] = coupling
    c = split(coupling)
    for at in range(0, 1024, 256):
        rows = slice(at, at + 256)
        o_ref[rows, :] = t_ref[rows, :] - dot3((bhi[rows, :], blo[rows, :]), c)


def finish(table, pieces, ihi, ilo, bhi, blo, trailing):
    depth, width = trailing.shape
    b = ihi.shape[0]
    return pl.pallas_call(
        finish_kernel,
        out_shape=(jax.ShapeDtypeStruct((b, width), F32), jax.ShapeDtypeStruct((depth, width), F32)),
        grid=(width // TILE,),
        in_specs=[SCALARS]
        + [pl.BlockSpec((64, TILE), lambda i: (0, i))] * 8
        + whole(4)
        + [pl.BlockSpec((depth, TILE), lambda i: (0, i))],
        out_specs=(pl.BlockSpec((b, TILE), lambda i: (0, i)), pl.BlockSpec((depth, TILE), lambda i: (0, i))),
        scratch_shapes=[pltpu.VMEM((b, TILE), F32)],
        compiler_params=params(48),
        name="finish",
    )(table, *pieces, ihi, ilo, bhi, blo, trailing)


def local(panel, trailing):
    row = lax.axis_index("row")
    core = row % 2
    bits = ring_bits(row // 2)
    rows, keep, give = gather_panel(panel, core)
    packed = sum_packed(keep, give, core)
    hi, lo = turn(rows)

    def held(part, i, j):
        s, t = (bits[0], bits[1]) if part == 0 else (bits[1], bits[0])
        return part * 4 + (i ^ s) * 2 + (j ^ t)

    spots = [held(part, i, j) for part in (0, 1) for i in (0, 1) for j in (0, 1)]
    give = share(jnp.stack([1 - core] + spots).astype(jnp.int32), hi, lo, trailing)
    keep = share(jnp.stack([core] + spots).astype(jnp.int32), hi, lo, trailing)
    got = swap(give, CORE)
    parts = [[keep[at:at + 64] + got[at:at + 64], keep[at + 64:at + 128] + got[at + 64:at + 128]] for at in (0, 128)]
    came = [swap(parts[h][1], XPAIR[h]) for h in (0, 1)]
    parts = [[parts[h][0][:32] + came[h][:32], parts[h][0][32:] + came[h][32:]] for h in (0, 1)]

    factors = [factor_rows(0, 4, [], packed)]
    factors.append(factor_rows(1, 4, factors, packed))
    parts, factors = lax.optimization_barrier((parts, factors))
    came = [swap(parts[h][1], XPAIR[1 - h]) for h in (0, 1)]
    own = [parts[h][0] + came[h] for h in (0, 1)]
    factors.append(factor_rows(2, 4, factors, packed))
    own, factors = lax.optimization_barrier((own, factors))
    came = [swap(own[h], XPAIR[1 - h]) for h in (0, 1)]
    own = [jnp.concatenate([own[h], came[h]], axis=0) for h in (0, 1)]
    factors.append(factor_rows(3, 4, factors, packed))
    own, factors = lax.optimization_barrier((own, factors))
    came = [swap(own[h], XPAIR[h]) for h in (0, 1)]
    r_factor, ihi, ilo, bhi, blo = prepare(factors, rows)
    mine = [own[0], came[0], own[1], came[1]]
    theirs = [swap(p, CORE) for p in mine]
    spots = [c * 8 + s for c in (core, 1 - core) for s in spots]
    coupling, out = finish(jnp.stack(spots).astype(jnp.int32), mine + theirs, ihi, ilo, bhi, blo, trailing)
    return (r_factor, coupling, out)


def solution(mesh):
    placed = (P(("row", "col"), None), P("row", "col"))
    return jax.shard_map(
        local,
        mesh=mesh,
        in_specs=placed,
        out_specs=(P(), P(None, "col"), P("row", "col")),
        check_vma=False,
    )
```

```python
import functools

import jax
import jax.numpy as jnp
from jax import lax
from jax.experimental import pallas as pl
from jax.experimental.pallas import tpu as pltpu
from jax.sharding import PartitionSpec as P

HIGHEST = lax.Precision.HIGHEST
BF16 = jnp.bfloat16
F32 = jnp.float32
GROUP = 32
TILE = 512
NARROW = 256


def near(i):
    return i ^ 1


def far(i):
    return 3 - i


CORE = [(r, r ^ 1) for r in range(8)]
XPAIR = [[(x * 2 + c, pair(x) * 2 + c) for x in range(4) for c in range(2)] for pair in (near, far)]


def ring_bits(i):
    return (i ^ (i // 2)) & 1, i // 2


def tdot(a, b, precision=HIGHEST):
    return lax.dot_general(a, b, (((0,), (0,)), ((), ())), precision=precision, preferred_element_type=F32)


def spread(v, s):
    return jnp.broadcast_to(v[s:s + 1, :], (8, 128))


def eliminate(slab, off, g):
    nt = g // 8
    width = slab.shape[1] // 128
    sub = lax.broadcasted_iota(jnp.int32, (8, 128), 0)
    rows = [[slab[8 * t:8 * t + 8, 128 * w:128 * w + 128] for w in range(width)] for t in range(nt)]
    cols = [
        [jnp.broadcast_to(rows[t][0][:, off + k:off + k + 1], (8, 128)) if t >= k // 8 else None for t in range(nt)]
        for k in range(g)
    ]
    scale = [None] * nt
    for j in range(g):
        tj, sj = divmod(j, 8)
        d = spread(cols[j][tj], sj)
        inv = 1.0 / d
        root = lax.rsqrt(d)
        scale[tj] = root if sj == 0 else jnp.where(sub >= sj, root, scale[tj])
        f = [None if t < tj else cols[j][t] * inv for t in range(nt)]
        for k in range(j + 1, g):
            a = spread(cols[j][k // 8], k % 8)
            for t in range(k // 8, nt):
                cols[k][t] = cols[k][t] - f[t] * a
        f[tj] = jnp.where(sub > sj, f[tj], 0.0)
        for w in range(width):
            p = spread(rows[tj][w], sj)
            for t in range(tj, nt):
                if t > tj or sj < 7:
                    rows[t][w] = rows[t][w] - f[t] * p
    return jnp.concatenate(
        [jnp.concatenate([rows[t][w] * scale[t] for w in range(width)], axis=1) for t in range(nt)], axis=0
    )


def params(mib=40):
    return pltpu.CompilerParams(vmem_limit_bytes=mib << 20)


def cheap():
    return pl.CostEstimate(flops=3 * 10 ** 8, bytes_accessed=10 ** 6, transcendentals=0)


def whole(n=1):
    return [pl.BlockSpec(memory_space=pltpu.VMEM)] * n


SCALARS = pl.BlockSpec(memory_space=pltpu.SMEM)


def split(a):
    high = a.astype(BF16)
    return high, (a - high.astype(F32)).astype(BF16)


def dot(a, b):
    return jnp.dot(a, b, preferred_element_type=F32)


def dot3(a, b):
    return dot(a[0], b[0]) + (dot(a[0], b[1]) + dot(a[1], b[0]))


def factor_kernel(k, nb, *refs):
    earlier, g_ref, w, m = refs[:k], refs[k], refs[k + 1], refs[k + 2]
    first = sum(nb - i for i in range(k)) * 128
    for j in range(nb - k):
        m[:, j * 128:j * 128 + 128] = g_ref[first + j * 128:first + j * 128 + 128, :]
    if k:
        m[:, (nb - k) * 128:nb * 128] = jnp.zeros((128, k * 128), F32)
    ri = lax.broadcasted_iota(jnp.int32, (128, 128), 0)
    ci = lax.broadcasted_iota(jnp.int32, (128, 128), 1)
    m[:, nb * 128:] = jnp.where(ri == ci, 1.0, 0.0)
    for i in range(k):
        at = (k - i) * 128
        known = earlier[i][:, at:]
        width = known.shape[1]
        m[:, :width] = m[:, :width] - tdot(earlier[i][:, at:at + 128], known)
    for q in range(128 // GROUP):
        lo, hi = q * GROUP, (q + 1) * GROUP
        slab = m[lo:hi, :]
        if q:
            slab = slab - tdot(w[0:lo, lo:hi], w[0:lo, :])
        w[lo:hi, :] = eliminate(slab, lo, GROUP)


def factor_rows(k, nb, earlier, packed):
    window = (nb + 1) * 128
    return pl.pallas_call(
        functools.partial(factor_kernel, k, nb),
        out_shape=jax.ShapeDtypeStruct((128, window), F32),
        in_specs=whole(k + 1),
        out_specs=whole()[0],
        scratch_shapes=[pltpu.VMEM((128, window), F32)],
        compiler_params=params(16),
        cost_estimate=cheap(),
        name="factor",
    )(*earlier, packed)


def shifts(axis):
    out = []
    for by in (1, 3, 2):
        if axis == "y":
            out.append((by, [(y * 4 + z, (y + by) % 4 * 4 + z) for y in range(4) for z in range(4)]))
        else:
            out.append((by, [(y * 4 + z, y * 4 + (z + by) % 4) for y in range(4) for z in range(4)]))
    return out


def gather_panel(panel):
    col = lax.axis_index("col")
    n = panel.shape[1] // 2
    held = [panel[:, :n], panel[:, n:]]
    place = [[(col // 4, col % 4)], [(col // 4, col % 4)]]
    pieces = [None, None]
    for step in (0, 1):
        for q in (0, 1):
            axis = "zy"[step ^ q]
            pieces[q] = [held[q]]
            known = list(place[q])
            for by, pairs in shifts(axis):
                pieces[q].append(lax.ppermute(held[q], "col", pairs))
                place[q] += [((y - by) % 4, z) if axis == "y" else (y, (z - by) % 4) for y, z in known]
        if step == 0:
            held = [jnp.concatenate(p, axis=0) for p in pieces]
    return pieces[0] + pieces[1], [y * 4 + z for q in (0, 1) for y, z in place[q]]


def turn_kernel(order_ref, *refs):
    pieces, (o_ref, hi_ref, lo_ref) = refs[:8], refs[8:]
    for i, ref in enumerate(pieces):
        q, four = divmod(i, 4)
        for p in range(4):
            at = pl.multiple_of(order_ref[i * 4 + p] * 64, 64)
            o_ref[pl.ds(at, 64), q * 256:q * 256 + 256] = ref[p * 64:p * 64 + 64, :]
    for j in range(0, 1024, 128):
        hi_ref[:, j:j + 128], lo_ref[:, j:j + 128] = split(jnp.transpose(o_ref[j:j + 128, :]))


def turn(pieces, order):
    depth, b = pieces[0].shape[0] * 4, pieces[0].shape[1] * 2
    out = jax.ShapeDtypeStruct((b, depth), BF16)
    return pl.pallas_call(
        turn_kernel,
        out_shape=(jax.ShapeDtypeStruct((depth, b), F32), out, out),
        in_specs=[SCALARS] + whole(8),
        out_specs=whole(3),
        compiler_params=params(),
        cost_estimate=cheap(),
        name="turn",
    )(jnp.stack(order).astype(jnp.int32), *pieces)


def gram_kernel(core_ref, p_ref, keep_ref, give_ref, blocks):
    at = 0
    for i in range(4):
        strip = tdot(p_ref[:, i * 128:i * 128 + 128], p_ref[:, i * 128:])
        for j in range(4 - i):
            blocks[at:at + 128, :] = strip[:, j * 128:j * 128 + 128]
            at += 128
    core = core_ref[0]
    keep_ref[...] = blocks[pl.ds(pl.multiple_of(core * 640, 128), 640), :]
    give_ref[...] = blocks[pl.ds(pl.multiple_of((1 - core) * 640, 128), 640), :]


def gram_share(rows, core):
    half = jax.ShapeDtypeStruct((640, 128), F32)
    return pl.pallas_call(
        gram_kernel,
        out_shape=(half, half),
        in_specs=[SCALARS] + whole(),
        out_specs=whole(2),
        scratch_shapes=[pltpu.VMEM((1280, 128), F32)],
        compiler_params=params(),
        cost_estimate=cheap(),
        name="gram",
    )(core.reshape(1).astype(jnp.int32), rows)


def join(own, other, bit):
    first = bit == 0
    return jnp.concatenate([jnp.where(first, own, other), jnp.where(first, other, own)], axis=0)


def swap(a, pairs):
    return lax.ppermute(a, "row", pairs)


def share_kernel(table_ref, hi_ref, lo_ref, t_ref, keep_ref, give_ref, total):
    got = dot3((hi_ref[...], lo_ref[...]), split(t_ref[...]))
    for p in range(16):
        at = pl.multiple_of(table_ref[p] * 32, 32)
        total[pl.ds(at, 32), :] = got[p * 32:p * 32 + 32, :]
    keep_ref[...] = total[:256, :]
    give_ref[...] = total[256:, :]


def share(table, hi, lo, trailing, first, width):
    depth = trailing.shape[0]
    half = jax.ShapeDtypeStruct((256, width), F32)
    out = pl.BlockSpec((256, TILE), lambda i: (0, i))
    return pl.pallas_call(
        share_kernel,
        out_shape=(half, half),
        grid=(width // TILE,),
        in_specs=[SCALARS] + whole(2) + [pl.BlockSpec((depth, TILE), lambda i: (0, i + first // TILE))],
        out_specs=(out, out),
        scratch_shapes=[pltpu.VMEM((512, TILE), F32)],
        compiler_params=params(),
        cost_estimate=cheap(),
        name="share",
    )(table, hi, lo, trailing)


def fold_kernel(k0, k1, g0, g1, a_give, b_give, a_keep, b_keep):
    n = k0.shape[1]
    for cols, k, g in ((slice(0, n), k0, g0), (slice(n, 2 * n), k1, g1)):
        for at, ref in ((64, a_give), (192, b_give), (0, a_keep), (128, b_keep)):
            ref[:, cols] = k[at:at + 64, :] + g[at:at + 64, :]


def fold(keeps, gots):
    out = jax.ShapeDtypeStruct((64, 2 * keeps[0].shape[1]), F32)
    return pl.pallas_call(
        fold_kernel,
        out_shape=(out,) * 4,
        in_specs=whole(4),
        out_specs=whole(4),
        compiler_params=params(),
        cost_estimate=cheap(),
        name="fold",
    )(*keeps, *gots)


def prepare_kernel(w0, w1, w2, w3, p_ref, r_ref, ihi_ref, ilo_ref, bhi_ref, blo_ref, inv):
    ri = lax.broadcasted_iota(jnp.int32, (128, 128), 0)
    ci = lax.broadcasted_iota(jnp.int32, (128, 128), 1)
    zero = jnp.zeros((128, 128), F32)
    for i, w in enumerate((w0, w1, w2, w3)):
        rows = slice(i * 128, i * 128 + 128)
        for j in range(4):
            cols = slice(j * 128, j * 128 + 128)
            if j < i:
                r_ref[rows, cols] = zero
            else:
                block = w[:, (j - i) * 128:(j - i) * 128 + 128]
                r_ref[rows, cols] = jnp.where(ri <= ci, block, 0.0) if j == i else block
            inv[rows, cols] = w[:, (4 - i + j) * 128:(5 - i + j) * 128] if j <= i else zero
    ihi_ref[...], ilo_ref[...] = split(inv[...])
    turned = split(jnp.transpose(inv[...]))
    for at in range(0, 1024, 256):
        rows = slice(at, at + 256)
        bhi_ref[rows, :], blo_ref[rows, :] = split(dot3(split(p_ref[rows, :]), turned))


def prepare(factors, rows):
    b = rows.shape[1]
    square, tall = (b, b), rows.shape
    return pl.pallas_call(
        prepare_kernel,
        out_shape=[jax.ShapeDtypeStruct(s, t) for s, t in ((square, F32), (square, BF16), (square, BF16), (tall, BF16), (tall, BF16))],
        in_specs=whole(5),
        out_specs=whole(5),
        scratch_shapes=[pltpu.VMEM(square, F32)],
        compiler_params=params(),
        cost_estimate=cheap(),
        name="prepare",
    )(*factors, rows)


def finish_kernel(table_ref, *refs):
    pieces, (ihi, ilo, bhi, blo, t_ref, c_ref, o_ref, total) = refs[:8], refs[8:]
    for p in range(8):
        for half in (0, 1):
            at = pl.multiple_of(table_ref[2 * p + half] * 32, 32)
            total[pl.ds(at, 32), :] = pieces[p][half * 32:half * 32 + 32, :]
    coupling = dot3((ihi[...], ilo[...]), split(total[...]))
    c_ref[...] = coupling
    c = split(coupling)
    for at in range(0, 1024, 256):
        rows = slice(at, at + 256)
        o_ref[rows, :] = t_ref[rows, :] - dot3((bhi[rows, :], blo[rows, :]), c)


def finish(table, pieces, ihi, ilo, bhi, blo, trailing):
    depth, width = trailing.shape
    b = ihi.shape[0]
    return pl.pallas_call(
        finish_kernel,
        out_shape=(jax.ShapeDtypeStruct((b, width), F32), jax.ShapeDtypeStruct((depth, width), F32)),
        grid=(width // NARROW,),
        in_specs=[SCALARS]
        + [pl.BlockSpec((64, NARROW), lambda i: (0, i))] * 8
        + whole(4)
        + [pl.BlockSpec((depth, NARROW), lambda i: (0, i))],
        out_specs=(pl.BlockSpec((b, NARROW), lambda i: (0, i)), pl.BlockSpec((depth, NARROW), lambda i: (0, i))),
        scratch_shapes=[pltpu.VMEM((b, NARROW), F32)],
        compiler_params=params(48),
        name="finish",
    )(table, *pieces, ihi, ilo, bhi, blo, trailing)


def after(value, *others):
    return lax.optimization_barrier((value, others))[0]


def local(panel, trailing):
    row = lax.axis_index("row")
    core = row % 2
    bits = ring_bits(row // 2)
    pieces, order = gather_panel(panel)
    rows, hi, lo = turn(pieces, order)

    def held(half, part, i, j):
        s, t = (bits[0], bits[1]) if part == 0 else (bits[1], bits[0])
        return (half ^ core) * 8 + part * 4 + (i ^ s) * 2 + (j ^ t)

    spots = [held(half, part, i, j) for half in (0, 1) for part in (0, 1) for i in (0, 1) for j in (0, 1)]
    table = jnp.stack(spots).astype(jnp.int32)
    width = trailing.shape[1] // 2
    keep, give = zip(*[share(table, hi, lo, trailing, at, width) for at in (0, width)])
    got = [swap(g, CORE) for g in give]
    a_give, b_give, a_keep, b_keep = fold(keep, got)

    came = [swap(g, XPAIR[h]) for h, g in ((0, a_give), (1, b_give))]
    gram_keep, gram_give = gram_share(after(rows, a_give), core)
    gram = gram_keep + swap(gram_give, CORE)
    n = gram.shape[0] // 2
    one, two = gram[:n], gram[n:]
    one, two = one + swap(one, XPAIR[0]), two + swap(two, XPAIR[1])

    parts = [(k[:32] + c[:32], k[32:] + c[32:]) for k, c in zip((a_keep, b_keep), came)]
    came = [swap(parts[h][1], XPAIR[1 - h]) for h in (0, 1)]
    one, two = one + swap(one, XPAIR[1]), two + swap(two, XPAIR[0])
    gram = jnp.concatenate([one, two], axis=0)
    packed = join(gram, swap(gram, CORE), core)

    own = [parts[h][0] + came[h] for h in (0, 1)]
    came = [swap(own[h], XPAIR[1 - h]) for h in (0, 1)]
    factors = [factor_rows(0, 4, [], packed)]
    factors.append(factor_rows(1, 4, factors, packed))
    own = [jnp.concatenate([own[h], came[h]], axis=0) for h in (0, 1)]
    own, factors = lax.optimization_barrier((own, factors))
    came = [swap(own[h], XPAIR[h]) for h in (0, 1)]
    factors.append(factor_rows(2, 4, factors, packed))
    factors.append(factor_rows(3, 4, factors, packed))
    r_factor, ihi, ilo, bhi, blo = prepare(factors, rows)
    came, ihi = lax.optimization_barrier((came, ihi))
    mine = [own[0], came[0], own[1], came[1]]
    theirs = [swap(p, CORE) for p in mine]
    coupling, out = finish(table, mine + theirs, ihi, ilo, bhi, blo, trailing)
    return (r_factor, coupling, out)


def solution(mesh):
    placed = (P(("row", "col"), None), P("row", "col"))
    return jax.shard_map(
        local,
        mesh=mesh,
        in_specs=placed,
        out_specs=(P(), P(None, "col"), P("row", "col")),
        check_vma=False,
    )
```

```python
import functools

import jax
import jax.numpy as jnp
from jax import lax
from jax.experimental import pallas as pl
from jax.experimental.pallas import tpu as pltpu
from jax.sharding import PartitionSpec as P

HIGHEST = lax.Precision.HIGHEST
BF16 = jnp.bfloat16
F32 = jnp.float32
GROUP = 32
TILE = 512


def near(i):
    return i ^ 1


def far(i):
    return 3 - i


PAIR = (near, far)
CORE = [(r, r ^ 1) for r in range(8)]
ROW = [[(x * 2 + c, PAIR[c ^ step](x) * 2 + c) for x in range(4) for c in (0, 1)] for step in (0, 1)]


def ring_bits(i):
    return (i ^ (i // 2)) & 1, i // 2


def tdot(a, b, precision=HIGHEST):
    return lax.dot_general(a, b, (((0,), (0,)), ((), ())), precision=precision, preferred_element_type=F32)


def spread(v, s):
    return jnp.broadcast_to(v[s:s + 1, :], (8, 128))


def eliminate(slab, off, g):
    nt = g // 8
    width = slab.shape[1] // 128
    sub = lax.broadcasted_iota(jnp.int32, (8, 128), 0)
    rows = [[slab[8 * t:8 * t + 8, 128 * w:128 * w + 128] for w in range(width)] for t in range(nt)]
    cols = [
        [jnp.broadcast_to(rows[t][0][:, off + k:off + k + 1], (8, 128)) if t >= k // 8 else None for t in range(nt)]
        for k in range(g)
    ]
    scale = [None] * nt
    for j in range(g):
        tj, sj = divmod(j, 8)
        d = spread(cols[j][tj], sj)
        inv = 1.0 / d
        root = lax.rsqrt(d)
        scale[tj] = root if sj == 0 else jnp.where(sub >= sj, root, scale[tj])
        f = [None if t < tj else cols[j][t] * inv for t in range(nt)]
        for k in range(j + 1, g):
            a = spread(cols[j][k // 8], k % 8)
            for t in range(k // 8, nt):
                cols[k][t] = cols[k][t] - f[t] * a
        f[tj] = jnp.where(sub > sj, f[tj], 0.0)
        for w in range(width):
            p = spread(rows[tj][w], sj)
            for t in range(tj, nt):
                if t > tj or sj < 7:
                    rows[t][w] = rows[t][w] - f[t] * p
    return jnp.concatenate(
        [jnp.concatenate([rows[t][w] * scale[t] for w in range(width)], axis=1) for t in range(nt)], axis=0
    )


def params(mib):
    return pltpu.CompilerParams(vmem_limit_bytes=mib << 20)


def cheap():
    return pl.CostEstimate(flops=3 * 10 ** 8, bytes_accessed=10 ** 6, transcendentals=0)


def whole(n=1):
    return [pl.BlockSpec(memory_space=pltpu.VMEM)] * n


SCALARS = pl.BlockSpec(memory_space=pltpu.SMEM)


def split(a):
    high = a.astype(BF16)
    return high, (a - high.astype(F32)).astype(BF16)


def dot(a, b):
    return jnp.dot(a, b, preferred_element_type=F32)


def dot3(a, b):
    return dot(a[0], b[0]) + (dot(a[0], b[1]) + dot(a[1], b[0]))


def factor_kernel(k, nb, *refs):
    earlier, g_ref, w, m = refs[:k], refs[k], refs[k + 1], refs[k + 2]
    first = sum(nb - i for i in range(k)) * 128
    for j in range(nb - k):
        m[:, j * 128:j * 128 + 128] = g_ref[first + j * 128:first + j * 128 + 128, :]
    if k:
        m[:, (nb - k) * 128:nb * 128] = jnp.zeros((128, k * 128), F32)
    ri = lax.broadcasted_iota(jnp.int32, (128, 128), 0)
    ci = lax.broadcasted_iota(jnp.int32, (128, 128), 1)
    m[:, nb * 128:] = jnp.where(ri == ci, 1.0, 0.0)
    for i in range(k):
        at = (k - i) * 128
        known = earlier[i][:, at:]
        width = known.shape[1]
        m[:, :width] = m[:, :width] - tdot(earlier[i][:, at:at + 128], known)
    for q in range(128 // GROUP):
        lo, hi = q * GROUP, (q + 1) * GROUP
        slab = m[lo:hi, :]
        if q:
            slab = slab - tdot(w[0:lo, lo:hi], w[0:lo, :])
        w[lo:hi, :] = eliminate(slab, lo, GROUP)


def factor_rows(k, nb, earlier, packed):
    window = (nb + 1) * 128
    return pl.pallas_call(
        functools.partial(factor_kernel, k, nb),
        out_shape=jax.ShapeDtypeStruct((128, window), F32),
        in_specs=whole(k + 1),
        out_specs=whole()[0],
        scratch_shapes=[pltpu.VMEM((128, window), F32)],
        compiler_params=params(8),
        cost_estimate=cheap(),
        name="factor",
    )(*earlier, packed)


def gather_pairs(q, step):
    out = []
    for x in range(4):
        for c in (0, 1):
            for y in range(4):
                for z in range(4):
                    flip = PAIR[(step % 2) ^ q]
                    to = (y, flip(z)) if (step // 2) ^ c == 0 else (flip(y), z)
                    out.append(((x * 2 + c) * 16 + y * 4 + z, (x * 2 + c) * 16 + to[0] * 4 + to[1]))
    return out


def gather_panel(panel, core):
    col = lax.axis_index("col")
    n = panel.shape[1] // 2
    pieces = [[panel[:, :n]], [panel[:, n:]]]
    place = [[(col // 4, col % 4)], [(col // 4, col % 4)]]
    for step in range(4):
        held = [p[0] if len(p) == 1 else jnp.concatenate(p, axis=0) for p in pieces]
        for q in (0, 1):
            pieces[q] = [held[q], lax.ppermute(held[q], ("row", "col"), gather_pairs(q, step))]
            flip = PAIR[(step % 2) ^ q]
            along_z = core == step // 2
            place[q] = place[q] + [
                (jnp.where(along_z, y, flip(y)), jnp.where(along_z, flip(z), z)) for y, z in place[q]
            ]
    return pieces[0] + pieces[1], [y * 4 + z for q in (0, 1) for y, z in place[q]]


def turn_kernel(order_ref, *refs):
    pieces, (o_ref, hi_ref, lo_ref) = refs[:4], refs[4:]
    for i, ref in enumerate(pieces):
        q = i // 2
        for p in range(8):
            at = pl.multiple_of(order_ref[i * 8 + p] * 64, 64)
            o_ref[pl.ds(at, 64), q * 256:q * 256 + 256] = ref[p * 64:p * 64 + 64, :]
    for j in range(0, 1024, 128):
        hi_ref[:, j:j + 128], lo_ref[:, j:j + 128] = split(jnp.transpose(o_ref[j:j + 128, :]))


def turn(pieces, order):
    depth, b = pieces[0].shape[0] * 2, pieces[0].shape[1] * 2
    out = jax.ShapeDtypeStruct((b, depth), BF16)
    return pl.pallas_call(
        turn_kernel,
        out_shape=(jax.ShapeDtypeStruct((depth, b), F32), out, out),
        in_specs=[SCALARS] + whole(4),
        out_specs=whole(3),
        compiler_params=params(12),
        cost_estimate=cheap(),
        name="turn",
    )(jnp.stack(order).astype(jnp.int32), *pieces)


def gram_kernel(core_ref, p_ref, keep_ref, give_ref, blocks):
    at = 0
    for i in range(4):
        strip = tdot(p_ref[:, i * 128:i * 128 + 128], p_ref[:, i * 128:])
        for j in range(4 - i):
            blocks[at:at + 128, :] = strip[:, j * 128:j * 128 + 128]
            at += 128
    core = core_ref[0]
    keep_ref[...] = blocks[pl.ds(pl.multiple_of(core * 640, 128), 640), :]
    give_ref[...] = blocks[pl.ds(pl.multiple_of((1 - core) * 640, 128), 640), :]


def gram_share(rows, core):
    half = jax.ShapeDtypeStruct((640, 128), F32)
    return pl.pallas_call(
        gram_kernel,
        out_shape=(half, half),
        in_specs=[SCALARS] + whole(),
        out_specs=whole(2),
        scratch_shapes=[pltpu.VMEM((1280, 128), F32)],
        compiler_params=params(12),
        cost_estimate=cheap(),
        name="gram",
    )(core.reshape(1).astype(jnp.int32), rows)


def join(own, other, bit):
    first = bit == 0
    return jnp.concatenate([jnp.where(first, own, other), jnp.where(first, other, own)], axis=0)


def swap(a, pairs):
    return lax.ppermute(a, "row", pairs)


def share_kernel(table_ref, hi_ref, lo_ref, t_ref, keep_ref, give_ref, total):
    got = dot3((hi_ref[...], lo_ref[...]), split(t_ref[...]))
    for p in range(8):
        at = pl.multiple_of(table_ref[p] * 64, 64)
        total[pl.ds(at, 64), :] = got[p * 64:p * 64 + 64, :]
    keep_ref[...] = total[:256, :]
    give_ref[...] = total[256:, :]


def share(table, hi, lo, trailing, first, width):
    depth = trailing.shape[0]
    half = jax.ShapeDtypeStruct((256, width), F32)
    out = pl.BlockSpec((256, TILE), lambda i: (0, i))
    return pl.pallas_call(
        share_kernel,
        out_shape=(half, half),
        grid=(width // TILE,),
        in_specs=[SCALARS] + whole(2) + [pl.BlockSpec((depth, TILE), lambda i: (0, i + first // TILE))],
        out_specs=(out, out),
        scratch_shapes=[pltpu.VMEM((512, TILE), F32)],
        compiler_params=params(58),
        cost_estimate=cheap(),
        name="share",
    )(table, hi, lo, trailing)


def fold_kernel(k0, k1, g0, g1, keep_ref, give_ref):
    n = k0.shape[1]
    for cols, k, g in ((slice(0, n), k0, g0), (slice(n, 2 * n), k1, g1)):
        give_ref[:, cols] = k[128:, :] + g[128:, :]
        keep_ref[:, cols] = k[:128, :] + g[:128, :]


def fold(keeps, gots):
    out = jax.ShapeDtypeStruct((128, 2 * keeps[0].shape[1]), F32)
    return pl.pallas_call(
        fold_kernel,
        out_shape=(out, out),
        in_specs=whole(4),
        out_specs=whole(2),
        compiler_params=params(12),
        cost_estimate=cheap(),
        name="fold",
    )(*keeps, *gots)


def prepare_kernel(w0, w1, w2, w3, p_ref, r_ref, ihi_ref, ilo_ref, bhi_ref, blo_ref, inv):
    ri = lax.broadcasted_iota(jnp.int32, (128, 128), 0)
    ci = lax.broadcasted_iota(jnp.int32, (128, 128), 1)
    zero = jnp.zeros((128, 128), F32)
    for i, w in enumerate((w0, w1, w2, w3)):
        rows = slice(i * 128, i * 128 + 128)
        for j in range(4):
            cols = slice(j * 128, j * 128 + 128)
            if j < i:
                r_ref[rows, cols] = zero
            else:
                block = w[:, (j - i) * 128:(j - i) * 128 + 128]
                r_ref[rows, cols] = jnp.where(ri <= ci, block, 0.0) if j == i else block
            inv[rows, cols] = w[:, (4 - i + j) * 128:(5 - i + j) * 128] if j <= i else zero
    ihi_ref[...], ilo_ref[...] = split(inv[...])
    turned = split(jnp.transpose(inv[...]))
    for at in range(0, 1024, 256):
        rows = slice(at, at + 256)
        bhi_ref[rows, :], blo_ref[rows, :] = split(dot3(split(p_ref[rows, :]), turned))


def prepare(factors, rows):
    b = rows.shape[1]
    square, tall = (b, b), rows.shape
    return pl.pallas_call(
        prepare_kernel,
        out_shape=[jax.ShapeDtypeStruct(s, t) for s, t in ((square, F32), (square, BF16), (square, BF16), (tall, BF16), (tall, BF16))],
        in_specs=whole(5),
        out_specs=whole(5),
        scratch_shapes=[pltpu.VMEM(square, F32)],
        compiler_params=params(16),
        cost_estimate=cheap(),
        name="prepare",
    )(*factors, rows)


def finish_kernel(table_ref, *refs):
    pieces, (ihi, ilo, bhi, blo, t_ref, c_ref, o_ref, total) = refs[:4], refs[4:]
    for p in range(8):
        at = pl.multiple_of(table_ref[p] * 64, 64)
        total[pl.ds(at, 64), :] = pieces[p // 2][p % 2 * 64:p % 2 * 64 + 64, :]
    coupling = dot3((ihi[...], ilo[...]), split(total[...]))
    c_ref[...] = coupling
    c = split(coupling)
    for at in range(0, 1024, 256):
        rows = slice(at, at + 256)
        o_ref[rows, :] = t_ref[rows, :] - dot3((bhi[rows, :], blo[rows, :]), c)


def finish(table, pieces, ihi, ilo, bhi, blo, trailing):
    depth, width = trailing.shape
    b = ihi.shape[0]
    return pl.pallas_call(
        finish_kernel,
        out_shape=(jax.ShapeDtypeStruct((b, width), F32), jax.ShapeDtypeStruct((depth, width), F32)),
        grid=(width // TILE,),
        in_specs=[SCALARS]
        + [pl.BlockSpec((128, TILE), lambda i: (0, i))] * 4
        + whole(4)
        + [pl.BlockSpec((depth, TILE), lambda i: (0, i))],
        out_specs=(pl.BlockSpec((b, TILE), lambda i: (0, i)), pl.BlockSpec((depth, TILE), lambda i: (0, i))),
        scratch_shapes=[pltpu.VMEM((b, TILE), F32)],
        compiler_params=params(58),
        name="finish",
    )(table, *pieces, ihi, ilo, bhi, blo, trailing)


def after(value, *others):
    return lax.optimization_barrier((value, others))[0]


def local(panel, trailing):
    row = lax.axis_index("row")
    core = row % 2
    bits = ring_bits(row // 2)
    pieces, order = gather_panel(panel, core)
    rows, hi, lo = turn(pieces, order)

    def held(half, i, j):
        owner = half ^ core
        return owner * 4 + (i ^ jnp.where(owner == 0, bits[0], bits[1])) * 2 + (j ^ jnp.where(owner == 0, bits[1], bits[0]))

    table = jnp.stack([held(half, i, j) for half in (0, 1) for i in (0, 1) for j in (0, 1)]).astype(jnp.int32)
    inverse = jnp.zeros_like(table).at[table].set(jnp.arange(8, dtype=jnp.int32))
    width = trailing.shape[1] // 2
    keep, give = zip(*[share(inverse, hi, lo, trailing, at, width) for at in (0, width)])
    keep, give = fold(keep, [swap(g, CORE) for g in give])

    came = swap(give, ROW[0])
    gram_keep, gram_give = gram_share(after(rows, give), core)
    gram = gram_keep + swap(gram_give, CORE)
    gram = gram + swap(gram, ROW[0])
    give, keep = keep[64:] + came[64:], keep[:64] + came[:64]
    came = swap(give, ROW[1])
    gram = gram + swap(gram, ROW[1])
    packed = join(gram, swap(gram, CORE), core)
    own = keep + came
    came = swap(own, ROW[1])
    factors = [factor_rows(0, 4, [], packed)]
    factors.append(factor_rows(1, 4, factors, packed))
    own = jnp.concatenate([own, came], axis=0)
    own, factors = lax.optimization_barrier((own, factors))
    came = swap(own, ROW[0])
    factors.append(factor_rows(2, 4, factors, packed))
    factors.append(factor_rows(3, 4, factors, packed))
    r_factor, ihi, ilo, bhi, blo = prepare(factors, rows)
    came, ihi = lax.optimization_barrier((came, ihi))
    mine = [own, came]
    theirs = [swap(p, CORE) for p in mine]
    coupling, out = finish(table, mine + theirs, ihi, ilo, bhi, blo, trailing)
    return (r_factor, coupling, out)


def solution(mesh):
    placed = (P(("row", "col"), None), P("row", "col"))
    return jax.shard_map(
        local,
        mesh=mesh,
        in_specs=placed,
        out_specs=(P(), P(None, "col"), P("row", "col")),
        check_vma=False,
    )
```

```python
import functools

import jax
import jax.numpy as jnp
from jax import lax
from jax.experimental import pallas as pl
from jax.experimental.pallas import tpu as pltpu
from jax.sharding import PartitionSpec as P

HIGHEST = lax.Precision.HIGHEST
BF16 = jnp.bfloat16
F32 = jnp.float32
GROUP = 32
TILE = 512


def near(i):
    return i ^ 1


def far(i):
    return 3 - i


PAIR = (near, far)
CORE = [(r, r ^ 1) for r in range(8)]
ROW = [[(x * 2 + c, PAIR[c ^ step](x) * 2 + c) for x in range(4) for c in (0, 1)] for step in (0, 1)]


def spots(row):
    core, x = row % 2, row // 2
    bits = ((x ^ (x // 2)) & 1, x // 2)
    out = []
    for half in (0, 1):
        owner = half ^ core
        one = jnp.where(owner == 0, bits[0], bits[1])
        two = jnp.where(owner == 0, bits[1], bits[0])
        out += [owner * 4 + (i ^ one) * 2 + (j ^ two) for i in (0, 1) for j in (0, 1)]
    return out


def places(core, col):
    out = []
    for q in (0, 1):
        place = [(col // 4, col % 4)]
        for step in range(4):
            flip = PAIR[(step % 2) ^ q]
            along_z = core == step // 2
            place = place + [(jnp.where(along_z, y, flip(y)), jnp.where(along_z, flip(z), z)) for y, z in place]
        out += [y * 4 + z for y, z in place]
    return out


def tdot(a, b, precision=HIGHEST):
    return lax.dot_general(a, b, (((0,), (0,)), ((), ())), precision=precision, preferred_element_type=F32)


def spread(v, s):
    return jnp.broadcast_to(v[s:s + 1, :], (8, 128))


def eliminate(slab, off, g):
    nt = g // 8
    width = slab.shape[1] // 128
    sub = lax.broadcasted_iota(jnp.int32, (8, 128), 0)
    rows = [[slab[8 * t:8 * t + 8, 128 * w:128 * w + 128] for w in range(width)] for t in range(nt)]
    cols = [
        [jnp.broadcast_to(rows[t][0][:, off + k:off + k + 1], (8, 128)) if t >= k // 8 else None for t in range(nt)]
        for k in range(g)
    ]
    scale = [None] * nt
    for j in range(g):
        tj, sj = divmod(j, 8)
        d = spread(cols[j][tj], sj)
        inv = 1.0 / d
        root = lax.rsqrt(d)
        scale[tj] = root if sj == 0 else jnp.where(sub >= sj, root, scale[tj])
        f = [None if t < tj else cols[j][t] * inv for t in range(nt)]
        for k in range(j + 1, g):
            a = spread(cols[j][k // 8], k % 8)
            for t in range(k // 8, nt):
                cols[k][t] = cols[k][t] - f[t] * a
        f[tj] = jnp.where(sub > sj, f[tj], 0.0)
        for w in range(width):
            p = spread(rows[tj][w], sj)
            for t in range(tj, nt):
                if t > tj or sj < 7:
                    rows[t][w] = rows[t][w] - f[t] * p
    return jnp.concatenate(
        [jnp.concatenate([rows[t][w] * scale[t] for w in range(width)], axis=1) for t in range(nt)], axis=0
    )


def params(mib):
    return pltpu.CompilerParams(vmem_limit_bytes=mib << 20)


def cheap(times=1):
    return pl.CostEstimate(flops=times * 3 * 10 ** 8, bytes_accessed=times * 10 ** 6, transcendentals=0)


def whole(n=1):
    return [pl.BlockSpec(memory_space=pltpu.VMEM)] * n


FAR = pl.BlockSpec(memory_space=pltpu.HBM)


def split(a):
    high = a.astype(BF16)
    return high, (a - high.astype(F32)).astype(BF16)


def dot(a, b):
    return jnp.dot(a, b, preferred_element_type=F32)


def dot3(a, b):
    return dot(a[0], b[0]) + (dot(a[0], b[1]) + dot(a[1], b[0]))


def factor_kernel(k, nb, *refs):
    earlier, (own, other, w, m) = refs[:k], refs[k:]
    core = lax.axis_index("row") % 2
    first = sum(nb - i for i in range(k))
    for j in range(nb - k):
        half, at = divmod(first + j, own.shape[0] // 128)
        rows = slice(at * 128, at * 128 + 128)
        m[:, j * 128:j * 128 + 128] = jnp.where(core == half, own[rows, :], other[rows, :])
    if k:
        m[:, (nb - k) * 128:nb * 128] = jnp.zeros((128, k * 128), F32)
    ri = lax.broadcasted_iota(jnp.int32, (128, 128), 0)
    ci = lax.broadcasted_iota(jnp.int32, (128, 128), 1)
    m[:, nb * 128:] = jnp.where(ri == ci, 1.0, 0.0)
    for i in range(k):
        at = (k - i) * 128
        known = earlier[i][:, at:]
        width = known.shape[1]
        m[:, :width] = m[:, :width] - tdot(earlier[i][:, at:at + 128], known)
    for q in range(128 // GROUP):
        lo, hi = q * GROUP, (q + 1) * GROUP
        slab = m[lo:hi, :]
        if q:
            slab = slab - tdot(w[0:lo, lo:hi], w[0:lo, :])
        w[lo:hi, :] = eliminate(slab, lo, GROUP)


def factor_rows(k, nb, earlier, packed):
    window = (nb + 1) * 128
    return pl.pallas_call(
        functools.partial(factor_kernel, k, nb),
        out_shape=jax.ShapeDtypeStruct((128, window), F32),
        in_specs=whole(k + 2),
        out_specs=whole()[0],
        scratch_shapes=[pltpu.VMEM((128, window), F32)],
        compiler_params=params(28),
        cost_estimate=cheap(),
        name="factor",
    )(*earlier, *packed)


def gather_pairs(q, step):
    out = []
    for x in range(4):
        for c in (0, 1):
            for y in range(4):
                for z in range(4):
                    flip = PAIR[(step % 2) ^ q]
                    to = (y, flip(z)) if (step // 2) ^ c == 0 else (flip(y), z)
                    out.append(((x * 2 + c) * 16 + y * 4 + z, (x * 2 + c) * 16 + to[0] * 4 + to[1]))
    return out


def gather_panel(panel):
    n = panel.shape[1] // 2
    pieces = [[panel[:, :n]], [panel[:, n:]]]
    for step in range(4):
        held = [p[0] if len(p) == 1 else jnp.concatenate(p, axis=0) for p in pieces]
        pieces = [[h, lax.ppermute(h, ("row", "col"), gather_pairs(q, step))] for q, h in enumerate(held)]
    return pieces[0] + pieces[1]


def turn_kernel(*refs):
    pieces, (o_ref, hi_ref, lo_ref) = refs[:4], refs[4:]
    order = places(lax.axis_index("row") % 2, lax.axis_index("col"))
    for i, ref in enumerate(pieces):
        q = i // 2
        for p in range(8):
            at = pl.multiple_of(order[i * 8 + p] * 64, 64)
            o_ref[pl.ds(at, 64), q * 256:q * 256 + 256] = ref[p * 64:p * 64 + 64, :]
    for j in range(0, 1024, 128):
        hi_ref[:, j:j + 128], lo_ref[:, j:j + 128] = split(jnp.transpose(o_ref[j:j + 128, :]))


def turn(pieces):
    depth, b = pieces[0].shape[0] * 2, pieces[0].shape[1] * 2
    out = jax.ShapeDtypeStruct((b, depth), BF16)
    return pl.pallas_call(
        turn_kernel,
        out_shape=(jax.ShapeDtypeStruct((depth, b), F32), out, out),
        in_specs=whole(4),
        out_specs=whole(3),
        compiler_params=params(28),
        cost_estimate=cheap(10),
        name="turn",
    )(*pieces)


def gram_kernel(p_ref, keep_ref, give_ref, blocks):
    at = 0
    for i in range(4):
        strip = tdot(p_ref[:, i * 128:i * 128 + 128], p_ref[:, i * 128:])
        for j in range(4 - i):
            blocks[at:at + 128, :] = strip[:, j * 128:j * 128 + 128]
            at += 128
    core = lax.axis_index("row") % 2
    keep_ref[...] = blocks[pl.ds(pl.multiple_of(core * 640, 128), 640), :]
    give_ref[...] = blocks[pl.ds(pl.multiple_of((1 - core) * 640, 128), 640), :]


def gram_share(rows):
    half = jax.ShapeDtypeStruct((640, 128), F32)
    return pl.pallas_call(
        gram_kernel,
        out_shape=(half, half),
        in_specs=whole(),
        out_specs=whole(2),
        scratch_shapes=[pltpu.VMEM((1280, 128), F32)],
        compiler_params=params(28),
        cost_estimate=cheap(10),
        name="gram",
    )(rows)


def swap(a, pairs):
    return lax.ppermute(a, "row", pairs)


def fetch(hbm, buf, sems, first):
    copies = []
    for i in range(buf.shape[0]):
        copies.append(pltpu.make_async_copy(hbm.at[:, pl.ds(first + i * TILE, TILE)], buf.at[i], sems.at[i]))
        copies[-1].start()
    return copies


def share_kernel(first, hi_ref, lo_ref, t_hbm, keep_ref, give_ref, buf, whole_share, sems):
    at_spot = spots(lax.axis_index("row"))
    for i, copy in enumerate(fetch(t_hbm, buf, sems, first)):
        copy.wait()
        whole_share[...] = dot3((hi_ref[...], lo_ref[...]), split(buf[i]))
        for p in range(8):
            block = pl.ds(pl.multiple_of(at_spot[p] * 64, 64), 64)
            ref = (keep_ref, give_ref)[p // 4]
            ref[p % 4 * 64:p % 4 * 64 + 64, i * TILE:i * TILE + TILE] = whole_share[block, :]


def share(hi, lo, trailing, first, width):
    depth = trailing.shape[0]
    half = jax.ShapeDtypeStruct((256, width), F32)
    return pl.pallas_call(
        functools.partial(share_kernel, first),
        out_shape=(half, half),
        in_specs=whole(2) + [FAR],
        out_specs=whole(2),
        scratch_shapes=[
            pltpu.VMEM((width // TILE, depth, TILE), F32),
            pltpu.VMEM((512, TILE), F32),
            pltpu.SemaphoreType.DMA((width // TILE,)),
        ],
        compiler_params=params(28),
        cost_estimate=cheap(10),
        name="share",
    )(hi, lo, trailing)


def fold_kernel(k0, k1, g0, g1, keep_ref, give_ref):
    n = k0.shape[1]
    for cols, k, g in ((slice(0, n), k0, g0), (slice(n, 2 * n), k1, g1)):
        give_ref[:, cols] = k[128:, :] + g[128:, :]
        keep_ref[:, cols] = k[:128, :] + g[:128, :]


def fold(keeps, gots):
    out = jax.ShapeDtypeStruct((128, 2 * keeps[0].shape[1]), F32)
    return pl.pallas_call(
        fold_kernel,
        out_shape=(out, out),
        in_specs=whole(4),
        out_specs=whole(2),
        compiler_params=params(28),
        cost_estimate=cheap(),
        name="fold",
    )(*keeps, *gots)


def prepare_kernel(w0, w1, w2, w3, p_ref, r_ref, ihi_ref, ilo_ref, bhi_ref, blo_ref, inv):
    ri = lax.broadcasted_iota(jnp.int32, (128, 128), 0)
    ci = lax.broadcasted_iota(jnp.int32, (128, 128), 1)
    zero = jnp.zeros((128, 128), F32)
    for i, w in enumerate((w0, w1, w2, w3)):
        rows = slice(i * 128, i * 128 + 128)
        for j in range(4):
            cols = slice(j * 128, j * 128 + 128)
            if j < i:
                r_ref[rows, cols] = zero
            else:
                block = w[:, (j - i) * 128:(j - i) * 128 + 128]
                r_ref[rows, cols] = jnp.where(ri <= ci, block, 0.0) if j == i else block
            inv[rows, cols] = w[:, (4 - i + j) * 128:(5 - i + j) * 128] if j <= i else zero
    ihi_ref[...], ilo_ref[...] = split(inv[...])
    turned = split(jnp.transpose(inv[...]))
    for at in range(0, 1024, 256):
        rows = slice(at, at + 256)
        bhi_ref[rows, :], blo_ref[rows, :] = split(dot3(split(p_ref[rows, :]), turned))


def prepare(factors, rows):
    b = rows.shape[1]
    square, tall = (b, b), rows.shape
    return pl.pallas_call(
        prepare_kernel,
        out_shape=[jax.ShapeDtypeStruct(s, t) for s, t in ((square, F32), (square, BF16), (square, BF16), (tall, BF16), (tall, BF16))],
        in_specs=whole(5),
        out_specs=whole(5),
        scratch_shapes=[pltpu.VMEM(square, F32)],
        compiler_params=params(28),
        cost_estimate=cheap(),
        name="prepare",
    )(*factors, rows)


def finish_kernel(first, *refs):
    pieces, (ihi, ilo, bhi, blo, t_hbm) = refs[:4], refs[4:9]
    c_hbm, o_hbm, buf, total, cbuf, in_sems, c_sems, o_sems = refs[-8:]
    n = total.shape[0] // 2
    at_spot = spots(lax.axis_index("row"))
    out = []
    for i, copy in enumerate(fetch(t_hbm, buf, in_sems, first)):
        cols = slice(i * TILE, i * TILE + TILE)
        for p in range(8):
            at = pl.multiple_of(at_spot[p] * 64, 64)
            total[pl.ds(at, 64), :] = pieces[p // 2][p % 2 * 64:p % 2 * 64 + 64, cols]
        high, low = split(total[...])
        for rows, depth in ((slice(0, n), n), (slice(n, 2 * n), 2 * n)):
            cbuf[i, rows, :] = dot3((ihi[rows, :depth], ilo[rows, :depth]), (high[:depth, :], low[:depth, :]))
        there = pl.ds(first + i * TILE, TILE)
        out.append(pltpu.make_async_copy(cbuf.at[i], c_hbm.at[:, there], c_sems.at[i]))
        out[-1].start()
        c = split(cbuf[i])
        copy.wait()
        for at in range(0, 1024, 512):
            rows = slice(at, at + 512)
            buf[i, rows, :] = buf[i, rows, :] - dot3((bhi[rows, :], blo[rows, :]), c)
            sem = o_sems.at[2 * i + at // 512]
            out.append(pltpu.make_async_copy(buf.at[i, pl.ds(at, 512), :], o_hbm.at[pl.ds(at, 512), there], sem))
            out[-1].start()
    for copy in out:
        copy.wait()


def finish(pieces, ihi, ilo, bhi, blo, trailing, first, done):
    depth, width = trailing.shape
    b = ihi.shape[0]
    tiles = pieces[0].shape[1] // TILE
    return pl.pallas_call(
        functools.partial(finish_kernel, first),
        out_shape=(jax.ShapeDtypeStruct((b, width), F32), jax.ShapeDtypeStruct((depth, width), F32)),
        in_specs=whole(8) + [FAR] * (1 + len(done)),
        out_specs=(FAR, FAR),
        scratch_shapes=[
            pltpu.VMEM((tiles, depth, TILE), F32),
            pltpu.VMEM((b, TILE), F32),
            pltpu.VMEM((tiles, b, TILE), F32),
            pltpu.SemaphoreType.DMA((tiles,)),
            pltpu.SemaphoreType.DMA((tiles,)),
            pltpu.SemaphoreType.DMA((2 * tiles,)),
        ],
        input_output_aliases={9 + i: i for i in range(len(done))},
        compiler_params=params(28),
        cost_estimate=cheap(),
        name="finish",
    )(*pieces, ihi, ilo, bhi, blo, trailing, *done)


def after(value, *others):
    return lax.optimization_barrier((value, others))[0]


def local(panel, trailing):
    rows, hi, lo = turn(gather_panel(panel))
    width = trailing.shape[1] // 2
    gram_keep, gram_give = gram_share(rows)
    gram_came = swap(gram_give, CORE)
    first = share(after(hi, gram_give), lo, trailing, 0, width)
    gram = gram_keep + gram_came
    came = swap(gram, ROW[0])
    second = share(after(hi, gram, first[0]), lo, trailing, width, width)
    gram = gram + came
    first, second, gram = lax.optimization_barrier((first, second, gram))
    came = swap(gram, ROW[1])
    keep, give = fold((first[0], second[0]), [swap(g, CORE) for g in (first[1], second[1])])

    x_came = swap(give, ROW[0])
    gram = gram + came
    packed = (gram, swap(gram, CORE))
    factors = [factor_rows(0, 4, [], packed)]
    factors.append(factor_rows(1, 4, factors, packed))
    keep, came, factors = lax.optimization_barrier((keep, x_came, factors))
    give, keep = keep[64:] + came[64:], keep[:64] + came[:64]
    came = swap(give, ROW[1])
    factors.append(factor_rows(2, 4, factors, packed))
    factors.append(factor_rows(3, 4, factors, packed))
    own, factors = lax.optimization_barrier((keep + came, factors))
    came = swap(own, ROW[1])
    r_factor, ihi, ilo, bhi, blo = prepare(factors, rows)
    own, came, ihi = lax.optimization_barrier((own, came, ihi))
    done = ()
    own = [jnp.concatenate([own[:, at:at + width], came[:, at:at + width]], axis=0) for at in (0, width)]
    came = [swap(p, ROW[0]) for p in own]
    own_across = [swap(p, CORE) for p in own]
    for c in (0, 1):
        pieces = [own[c], came[c], own_across[c], swap(came[c], CORE)]
        done = finish(pieces, ihi, ilo, bhi, blo, trailing, c * width, done)
        if c == 0:
            done, came = lax.optimization_barrier((done, came))
    return (r_factor, *done)


def solution(mesh):
    placed = (P(("row", "col"), None), P("row", "col"))
    return jax.shard_map(
        local,
        mesh=mesh,
        in_specs=placed,
        out_specs=(P(), P(None, "col"), P("row", "col")),
        check_vma=False,
    )
```

```python
import functools

import jax
import jax.numpy as jnp
from jax import lax
from jax.experimental import pallas as pl
from jax.experimental.pallas import tpu as pltpu
from jax.sharding import PartitionSpec as P

HIGHEST = lax.Precision.HIGHEST
BF16 = jnp.bfloat16
F32 = jnp.float32
GROUP = 32
TILE = 512


def near(i):
    return i ^ 1


def far(i):
    return 3 - i


PAIR = (near, far)
CORE = [(r, r ^ 1) for r in range(8)]
ROW = [[(x * 2 + c, PAIR[c ^ step](x) * 2 + c) for x in range(4) for c in (0, 1)] for step in (0, 1)]


def spots(row):
    core, x = row % 2, row // 2
    bits = ((x ^ (x // 2)) & 1, x // 2)
    out = []
    for half in (0, 1):
        owner = half ^ core
        one = jnp.where(owner == 0, bits[0], bits[1])
        two = jnp.where(owner == 0, bits[1], bits[0])
        out += [owner * 4 + (i ^ one) * 2 + (j ^ two) for i in (0, 1) for j in (0, 1)]
    return out


def places(core, col):
    out = []
    for q in (0, 1):
        place = [(col // 4, col % 4)]
        for step in range(4):
            flip = PAIR[(step % 2) ^ q]
            along_z = core == step // 2
            place = place + [(jnp.where(along_z, y, flip(y)), jnp.where(along_z, flip(z), z)) for y, z in place]
        out += [y * 4 + z for y, z in place]
    return out


def tdot(a, b, precision=HIGHEST):
    return lax.dot_general(a, b, (((0,), (0,)), ((), ())), precision=precision, preferred_element_type=F32)


def spread(v, s):
    return jnp.broadcast_to(v[s:s + 1, :], (8, 128))


def eliminate(slab, off, g):
    nt = g // 8
    width = slab.shape[1] // 128
    sub = lax.broadcasted_iota(jnp.int32, (8, 128), 0)
    rows = [[slab[8 * t:8 * t + 8, 128 * w:128 * w + 128] for w in range(width)] for t in range(nt)]
    cols = [
        [jnp.broadcast_to(rows[t][0][:, off + k:off + k + 1], (8, 128)) if t >= k // 8 else None for t in range(nt)]
        for k in range(g)
    ]
    scale = [None] * nt
    for j in range(g):
        tj, sj = divmod(j, 8)
        d = spread(cols[j][tj], sj)
        inv = 1.0 / d
        root = lax.rsqrt(d)
        scale[tj] = root if sj == 0 else jnp.where(sub >= sj, root, scale[tj])
        f = [None if t < tj else cols[j][t] * inv for t in range(nt)]
        for k in range(j + 1, g):
            a = spread(cols[j][k // 8], k % 8)
            for t in range(k // 8, nt):
                cols[k][t] = cols[k][t] - f[t] * a
        f[tj] = jnp.where(sub > sj, f[tj], 0.0)
        for w in range(width):
            p = spread(rows[tj][w], sj)
            for t in range(tj, nt):
                if t > tj or sj < 7:
                    rows[t][w] = rows[t][w] - f[t] * p
    return jnp.concatenate(
        [jnp.concatenate([rows[t][w] * scale[t] for w in range(width)], axis=1) for t in range(nt)], axis=0
    )


def params(mib):
    return pltpu.CompilerParams(vmem_limit_bytes=mib << 20)


def cheap(times=1):
    return pl.CostEstimate(flops=times * 3 * 10 ** 8, bytes_accessed=times * 10 ** 6, transcendentals=0)


def whole(n=1):
    return [pl.BlockSpec(memory_space=pltpu.VMEM)] * n


FAR = pl.BlockSpec(memory_space=pltpu.HBM)


def split(a):
    high = a.astype(BF16)
    return high, (a - high.astype(F32)).astype(BF16)


def dot(a, b):
    return jnp.dot(a, b, preferred_element_type=F32)


def dot3(a, b):
    return dot(a[0], b[0]) + (dot(a[0], b[1]) + dot(a[1], b[0]))


def factor_kernel(k, nb, *refs):
    earlier, (own, other, w, m) = refs[:k], refs[k:]
    core = lax.axis_index("row") % 2
    first = sum(nb - i for i in range(k))
    for j in range(nb - k):
        half, at = divmod(first + j, own.shape[0] // 128)
        rows = slice(at * 128, at * 128 + 128)
        m[:, j * 128:j * 128 + 128] = jnp.where(core == half, own[rows, :], other[rows, :])
    if k:
        m[:, (nb - k) * 128:nb * 128] = jnp.zeros((128, k * 128), F32)
    ri = lax.broadcasted_iota(jnp.int32, (128, 128), 0)
    ci = lax.broadcasted_iota(jnp.int32, (128, 128), 1)
    m[:, nb * 128:] = jnp.where(ri == ci, 1.0, 0.0)
    for i in range(k):
        at = (k - i) * 128
        known = earlier[i][:, at:]
        width = known.shape[1]
        m[:, :width] = m[:, :width] - tdot(earlier[i][:, at:at + 128], known)
    for q in range(128 // GROUP):
        lo, hi = q * GROUP, (q + 1) * GROUP
        slab = m[lo:hi, :]
        if q:
            slab = slab - tdot(w[0:lo, lo:hi], w[0:lo, :])
        w[lo:hi, :] = eliminate(slab, lo, GROUP)


def factor_rows(k, nb, earlier, packed):
    window = (nb + 1) * 128
    return pl.pallas_call(
        functools.partial(factor_kernel, k, nb),
        out_shape=jax.ShapeDtypeStruct((128, window), F32),
        in_specs=whole(k + 2),
        out_specs=whole()[0],
        scratch_shapes=[pltpu.VMEM((128, window), F32)],
        compiler_params=params(28),
        cost_estimate=cheap(),
        name="factor",
    )(*earlier, *packed)


def gather_pairs(q, step):
    out = []
    for x in range(4):
        for c in (0, 1):
            for y in range(4):
                for z in range(4):
                    flip = PAIR[(step % 2) ^ q]
                    to = (y, flip(z)) if (step // 2) ^ c == 0 else (flip(y), z)
                    out.append(((x * 2 + c) * 16 + y * 4 + z, (x * 2 + c) * 16 + to[0] * 4 + to[1]))
    return out


def gather_panel(panel):
    n = panel.shape[1] // 2
    pieces = [[panel[:, :n]], [panel[:, n:]]]
    for step in range(4):
        held = [p[0] if len(p) == 1 else jnp.concatenate(p, axis=0) for p in pieces]
        pieces = [[h, lax.ppermute(h, ("row", "col"), gather_pairs(q, step))] for q, h in enumerate(held)]
    return pieces[0] + pieces[1]


def turn_kernel(*refs):
    pieces, (o_ref, hi_ref, lo_ref) = refs[:4], refs[4:]
    order = places(lax.axis_index("row") % 2, lax.axis_index("col"))
    for i, ref in enumerate(pieces):
        q = i // 2
        for p in range(8):
            at = pl.multiple_of(order[i * 8 + p] * 64, 64)
            o_ref[pl.ds(at, 64), q * 256:q * 256 + 256] = ref[p * 64:p * 64 + 64, :]
    for j in range(0, 1024, 128):
        hi_ref[:, j:j + 128], lo_ref[:, j:j + 128] = split(jnp.transpose(o_ref[j:j + 128, :]))


def turn(pieces):
    depth, b = pieces[0].shape[0] * 2, pieces[0].shape[1] * 2
    out = jax.ShapeDtypeStruct((b, depth), BF16)
    return pl.pallas_call(
        turn_kernel,
        out_shape=(jax.ShapeDtypeStruct((depth, b), F32), out, out),
        in_specs=whole(4),
        out_specs=whole(3),
        compiler_params=params(28),
        cost_estimate=cheap(10),
        name="turn",
    )(*pieces)


def gram_kernel(p_ref, keep_ref, give_ref, blocks):
    at = 0
    for i in range(4):
        strip = tdot(p_ref[:, i * 128:i * 128 + 128], p_ref[:, i * 128:])
        for j in range(4 - i):
            blocks[at:at + 128, :] = strip[:, j * 128:j * 128 + 128]
            at += 128
    core = lax.axis_index("row") % 2
    keep_ref[...] = blocks[pl.ds(pl.multiple_of(core * 640, 128), 640), :]
    give_ref[...] = blocks[pl.ds(pl.multiple_of((1 - core) * 640, 128), 640), :]


def gram_share(rows):
    half = jax.ShapeDtypeStruct((640, 128), F32)
    return pl.pallas_call(
        gram_kernel,
        out_shape=(half, half),
        in_specs=whole(),
        out_specs=whole(2),
        scratch_shapes=[pltpu.VMEM((1280, 128), F32)],
        compiler_params=params(28),
        cost_estimate=cheap(10),
        name="gram",
    )(rows)


def swap(a, pairs):
    return lax.ppermute(a, "row", pairs)


def fetch(hbm, buf, sems, first):
    copies = []
    for i in range(buf.shape[0]):
        copies.append(pltpu.make_async_copy(hbm.at[:, pl.ds(first + i * TILE, TILE)], buf.at[i], sems.at[i]))
        copies[-1].start()
    return copies


def share_kernel(first, hi_ref, lo_ref, t_hbm, keep_ref, give_ref, buf, whole_share, sems):
    at_spot = spots(lax.axis_index("row"))
    for i, copy in enumerate(fetch(t_hbm, buf, sems, first)):
        copy.wait()
        whole_share[...] = dot3((hi_ref[...], lo_ref[...]), split(buf[i]))
        for p in range(8):
            block = pl.ds(pl.multiple_of(at_spot[p] * 64, 64), 64)
            ref = (keep_ref, give_ref)[p // 4]
            ref[p % 4 * 64:p % 4 * 64 + 64, i * TILE:i * TILE + TILE] = whole_share[block, :]


def share(hi, lo, trailing, first, width):
    depth = trailing.shape[0]
    half = jax.ShapeDtypeStruct((256, width), F32)
    return pl.pallas_call(
        functools.partial(share_kernel, first),
        out_shape=(half, half),
        in_specs=whole(2) + [FAR],
        out_specs=whole(2),
        scratch_shapes=[
            pltpu.VMEM((width // TILE, depth, TILE), F32),
            pltpu.VMEM((512, TILE), F32),
            pltpu.SemaphoreType.DMA((width // TILE,)),
        ],
        compiler_params=params(28),
        cost_estimate=cheap(10),
        name="share",
    )(hi, lo, trailing)


def fold_kernel(k0, k1, g0, g1, keep_ref, give_ref):
    n = k0.shape[1]
    for cols, k, g in ((slice(0, n), k0, g0), (slice(n, 2 * n), k1, g1)):
        give_ref[:, cols] = k[128:, :] + g[128:, :]
        keep_ref[:, cols] = k[:128, :] + g[:128, :]


def fold(keeps, gots):
    out = jax.ShapeDtypeStruct((128, 2 * keeps[0].shape[1]), F32)
    return pl.pallas_call(
        fold_kernel,
        out_shape=(out, out),
        in_specs=whole(4),
        out_specs=whole(2),
        compiler_params=params(28),
        cost_estimate=cheap(),
        name="fold",
    )(*keeps, *gots)


def prepare_kernel(w0, w1, w2, w3, p_ref, r_ref, ihi_ref, ilo_ref, bhi_ref, blo_ref, inv):
    ri = lax.broadcasted_iota(jnp.int32, (128, 128), 0)
    ci = lax.broadcasted_iota(jnp.int32, (128, 128), 1)
    zero = jnp.zeros((128, 128), F32)
    for i, w in enumerate((w0, w1, w2, w3)):
        rows = slice(i * 128, i * 128 + 128)
        for j in range(4):
            cols = slice(j * 128, j * 128 + 128)
            if j < i:
                r_ref[rows, cols] = zero
            else:
                block = w[:, (j - i) * 128:(j - i) * 128 + 128]
                r_ref[rows, cols] = jnp.where(ri <= ci, block, 0.0) if j == i else block
            inv[rows, cols] = w[:, (4 - i + j) * 128:(5 - i + j) * 128] if j <= i else zero
    ihi_ref[...], ilo_ref[...] = split(inv[...])
    turned = split(jnp.transpose(inv[...]))
    for at in range(0, 1024, 256):
        rows = slice(at, at + 256)
        bhi_ref[rows, :], blo_ref[rows, :] = split(dot3(split(p_ref[rows, :]), turned))


def prepare(factors, rows):
    b = rows.shape[1]
    square, tall = (b, b), rows.shape
    return pl.pallas_call(
        prepare_kernel,
        out_shape=[jax.ShapeDtypeStruct(s, t) for s, t in ((square, F32), (square, BF16), (square, BF16), (tall, BF16), (tall, BF16))],
        in_specs=whole(5),
        out_specs=whole(5),
        scratch_shapes=[pltpu.VMEM(square, F32)],
        compiler_params=params(28),
        cost_estimate=cheap(),
        name="prepare",
    )(*factors, rows)


def finish_kernel(first, *refs):
    pieces, (ihi, ilo, bhi, blo, t_hbm) = refs[:4], refs[4:9]
    c_hbm, o_hbm, buf, total, cbuf, in_sems, c_sems, o_sems = refs[-8:]
    n = total.shape[0] // 2
    at_spot = spots(lax.axis_index("row"))
    out = []
    for i, copy in enumerate(fetch(t_hbm, buf, in_sems, first)):
        cols = slice(i * TILE, i * TILE + TILE)
        for p in range(8):
            at = pl.multiple_of(at_spot[p] * 64, 64)
            total[pl.ds(at, 64), :] = pieces[p // 2][p % 2 * 64:p % 2 * 64 + 64, cols]
        high, low = split(total[...])
        for rows, depth in ((slice(0, n), n), (slice(n, 2 * n), 2 * n)):
            cbuf[i, rows, :] = dot3((ihi[rows, :depth], ilo[rows, :depth]), (high[:depth, :], low[:depth, :]))
        there = pl.ds(first + i * TILE, TILE)
        out.append(pltpu.make_async_copy(cbuf.at[i], c_hbm.at[:, there], c_sems.at[i]))
        out[-1].start()
        c = split(cbuf[i])
        copy.wait()
        for at in range(0, 1024, 512):
            rows = slice(at, at + 512)
            buf[i, rows, :] = buf[i, rows, :] - dot3((bhi[rows, :], blo[rows, :]), c)
            sem = o_sems.at[2 * i + at // 512]
            out.append(pltpu.make_async_copy(buf.at[i, pl.ds(at, 512), :], o_hbm.at[pl.ds(at, 512), there], sem))
            out[-1].start()
    for copy in out:
        copy.wait()


def finish(pieces, ihi, ilo, bhi, blo, trailing, first, done):
    depth, width = trailing.shape
    b = ihi.shape[0]
    tiles = pieces[0].shape[1] // TILE
    return pl.pallas_call(
        functools.partial(finish_kernel, first),
        out_shape=(jax.ShapeDtypeStruct((b, width), F32), jax.ShapeDtypeStruct((depth, width), F32)),
        in_specs=whole(8) + [FAR] * (1 + len(done)),
        out_specs=(FAR, FAR),
        scratch_shapes=[
            pltpu.VMEM((tiles, depth, TILE), F32),
            pltpu.VMEM((b, TILE), F32),
            pltpu.VMEM((tiles, b, TILE), F32),
            pltpu.SemaphoreType.DMA((tiles,)),
            pltpu.SemaphoreType.DMA((tiles,)),
            pltpu.SemaphoreType.DMA((2 * tiles,)),
        ],
        input_output_aliases={9 + i: i for i in range(len(done))},
        compiler_params=params(28),
        cost_estimate=cheap(),
        name="finish",
    )(*pieces, ihi, ilo, bhi, blo, trailing, *done)


def after(value, *others):
    return lax.optimization_barrier((value, others))[0]


def local(panel, trailing):
    rows, hi, lo = turn(gather_panel(panel))
    width = trailing.shape[1] // 2
    gram_keep, gram_give = gram_share(rows)
    gram_came = swap(gram_give, CORE)
    gram = gram_keep + gram_came
    came = swap(gram, ROW[0])
    first = share(after(hi, gram), lo, trailing, 0, width)
    gram = after(gram, first[0]) + came
    came = swap(gram, ROW[1])
    second = share(after(hi, gram, first[0]), lo, trailing, width, width)
    gram = gram + came
    second, gram = lax.optimization_barrier((second, gram))
    keep, give = fold((first[0], second[0]), [swap(g, CORE) for g in (first[1], second[1])])

    x_came = swap(give, ROW[0])
    packed = (gram, swap(gram, CORE))
    factors = [factor_rows(0, 4, [], packed)]
    factors.append(factor_rows(1, 4, factors, packed))
    keep, came, factors = lax.optimization_barrier((keep, x_came, factors))
    give, keep = keep[64:] + came[64:], keep[:64] + came[:64]
    came = swap(give, ROW[1])
    factors.append(factor_rows(2, 4, factors, packed))
    factors.append(factor_rows(3, 4, factors, packed))
    own, factors = lax.optimization_barrier((keep + came, factors))
    came = swap(own, ROW[1])
    r_factor, ihi, ilo, bhi, blo = prepare(factors, rows)
    own, came, ihi = lax.optimization_barrier((own, came, ihi))
    done = ()
    own = [jnp.concatenate([own[:, at:at + width], came[:, at:at + width]], axis=0) for at in (0, width)]
    came = [swap(own[0], ROW[0])]
    own[1] = after(own[1], came[0])
    came.append(swap(own[1], ROW[0]))
    own_across = [swap(p, CORE) for p in own]
    for c in (0, 1):
        pieces = [own[c], came[c], own_across[c], swap(came[c], CORE)]
        done = finish(pieces, ihi, ilo, bhi, blo, trailing, c * width, done)
        if c == 0:
            done, came = lax.optimization_barrier((done, came))
    return (r_factor, *done)


def solution(mesh):
    placed = (P(("row", "col"), None), P("row", "col"))
    return jax.shard_map(
        local,
        mesh=mesh,
        in_specs=placed,
        out_specs=(P(), P(None, "col"), P("row", "col")),
        check_vma=False,
    )
```

```python
import functools

import jax
import jax.numpy as jnp
from jax import lax
from jax.experimental import pallas as pl
from jax.experimental.pallas import tpu as pltpu
from jax.sharding import PartitionSpec as P

HIGHEST = lax.Precision.HIGHEST
BF16 = jnp.bfloat16
F32 = jnp.float32
GROUP = 32
TILE = 512


def near(i):
    return i ^ 1


def far(i):
    return 3 - i


PAIR = (near, far)
CORE = [(r, r ^ 1) for r in range(8)]
ROW = [[(x * 2 + c, PAIR[c ^ step](x) * 2 + c) for x in range(4) for c in (0, 1)] for step in (0, 1)]


def spots(row):
    core, x = row % 2, row // 2
    bits = ((x ^ (x // 2)) & 1, x // 2)
    out = []
    for half in (0, 1):
        owner = half ^ core
        one = jnp.where(owner == 0, bits[0], bits[1])
        two = jnp.where(owner == 0, bits[1], bits[0])
        out += [owner * 4 + (i ^ one) * 2 + (j ^ two) for i in (0, 1) for j in (0, 1)]
    return out


def places(core, col):
    out = []
    for q in (0, 1):
        place = [(col // 4, col % 4)]
        for step in range(4):
            flip = PAIR[(step % 2) ^ q]
            along_z = core == step // 2
            place = place + [(jnp.where(along_z, y, flip(y)), jnp.where(along_z, flip(z), z)) for y, z in place]
        out += [y * 4 + z for y, z in place]
    return out


def tdot(a, b, precision=HIGHEST):
    return lax.dot_general(a, b, (((0,), (0,)), ((), ())), precision=precision, preferred_element_type=F32)


def spread(v, s):
    return jnp.broadcast_to(v[s:s + 1, :], (8, 128))


def eliminate(slab, off, g):
    nt = g // 8
    width = slab.shape[1] // 128
    sub = lax.broadcasted_iota(jnp.int32, (8, 128), 0)
    rows = [[slab[8 * t:8 * t + 8, 128 * w:128 * w + 128] for w in range(width)] for t in range(nt)]
    cols = [
        [jnp.broadcast_to(rows[t][0][:, off + k:off + k + 1], (8, 128)) if t >= k // 8 else None for t in range(nt)]
        for k in range(g)
    ]
    scale = [None] * nt
    for j in range(g):
        tj, sj = divmod(j, 8)
        d = spread(cols[j][tj], sj)
        inv = 1.0 / d
        root = lax.rsqrt(d)
        scale[tj] = root if sj == 0 else jnp.where(sub >= sj, root, scale[tj])
        f = [None if t < tj else cols[j][t] * inv for t in range(nt)]
        for k in range(j + 1, g):
            a = spread(cols[j][k // 8], k % 8)
            for t in range(k // 8, nt):
                cols[k][t] = cols[k][t] - f[t] * a
        f[tj] = jnp.where(sub > sj, f[tj], 0.0)
        for w in range(width):
            p = spread(rows[tj][w], sj)
            for t in range(tj, nt):
                if t > tj or sj < 7:
                    rows[t][w] = rows[t][w] - f[t] * p
    return jnp.concatenate(
        [jnp.concatenate([rows[t][w] * scale[t] for w in range(width)], axis=1) for t in range(nt)], axis=0
    )


def params(mib):
    return pltpu.CompilerParams(vmem_limit_bytes=mib << 20)


def cheap(times=1):
    return pl.CostEstimate(flops=times * 3 * 10 ** 8, bytes_accessed=times * 10 ** 6, transcendentals=0)


def whole(n=1):
    return [pl.BlockSpec(memory_space=pltpu.VMEM)] * n


FAR = pl.BlockSpec(memory_space=pltpu.HBM)


def split(a):
    high = a.astype(BF16)
    return high, (a - high.astype(F32)).astype(BF16)


def dot(a, b):
    return jnp.dot(a, b, preferred_element_type=F32)


def dot3(a, b):
    return dot(a[0], b[0]) + (dot(a[0], b[1]) + dot(a[1], b[0]))


def factor_kernel(k, nb, *refs):
    earlier, (own, other, w, m) = refs[:k], refs[k:]
    core = lax.axis_index("row") % 2
    first = sum(nb - i for i in range(k))
    for j in range(nb - k):
        half, at = divmod(first + j, own.shape[0] // 128)
        rows = slice(at * 128, at * 128 + 128)
        m[:, j * 128:j * 128 + 128] = jnp.where(core == half, own[rows, :], other[rows, :])
    if k:
        m[:, (nb - k) * 128:nb * 128] = jnp.zeros((128, k * 128), F32)
    ri = lax.broadcasted_iota(jnp.int32, (128, 128), 0)
    ci = lax.broadcasted_iota(jnp.int32, (128, 128), 1)
    m[:, nb * 128:] = jnp.where(ri == ci, 1.0, 0.0)
    for i in range(k):
        at = (k - i) * 128
        known = earlier[i][:, at:]
        width = known.shape[1]
        m[:, :width] = m[:, :width] - tdot(earlier[i][:, at:at + 128], known)
    for q in range(128 // GROUP):
        lo, hi = q * GROUP, (q + 1) * GROUP
        slab = m[lo:hi, :]
        if q:
            slab = slab - tdot(w[0:lo, lo:hi], w[0:lo, :])
        w[lo:hi, :] = eliminate(slab, lo, GROUP)


def factor_rows(k, nb, earlier, packed):
    window = (nb + 1) * 128
    return pl.pallas_call(
        functools.partial(factor_kernel, k, nb),
        out_shape=jax.ShapeDtypeStruct((128, window), F32),
        in_specs=whole(k + 2),
        out_specs=whole()[0],
        scratch_shapes=[pltpu.VMEM((128, window), F32)],
        compiler_params=params(28),
        cost_estimate=cheap(),
        name="factor",
    )(*earlier, *packed)


def gather_pairs(q, step):
    out = []
    for x in range(4):
        for c in (0, 1):
            for y in range(4):
                for z in range(4):
                    flip = PAIR[(step % 2) ^ q]
                    to = (y, flip(z)) if (step // 2) ^ c == 0 else (flip(y), z)
                    out.append(((x * 2 + c) * 16 + y * 4 + z, (x * 2 + c) * 16 + to[0] * 4 + to[1]))
    return out


def gather_panel(panel):
    n = panel.shape[1] // 2
    pieces = [[panel[:, :n]], [panel[:, n:]]]
    for step in range(4):
        held = [p[0] if len(p) == 1 else jnp.concatenate(p, axis=0) for p in pieces]
        pieces = [[h, lax.ppermute(h, ("row", "col"), gather_pairs(q, step))] for q, h in enumerate(held)]
    return pieces[0] + pieces[1]


def turn_kernel(*refs):
    pieces, (o_ref, hi_ref, lo_ref) = refs[:4], refs[4:]
    order = places(lax.axis_index("row") % 2, lax.axis_index("col"))
    for i, ref in enumerate(pieces):
        q = i // 2
        for p in range(8):
            at = pl.multiple_of(order[i * 8 + p] * 64, 64)
            o_ref[pl.ds(at, 64), q * 256:q * 256 + 256] = ref[p * 64:p * 64 + 64, :]
    for j in range(0, 1024, 128):
        hi_ref[:, j:j + 128], lo_ref[:, j:j + 128] = split(jnp.transpose(o_ref[j:j + 128, :]))


def turn(pieces):
    depth, b = pieces[0].shape[0] * 2, pieces[0].shape[1] * 2
    out = jax.ShapeDtypeStruct((b, depth), BF16)
    return pl.pallas_call(
        turn_kernel,
        out_shape=(jax.ShapeDtypeStruct((depth, b), F32), out, out),
        in_specs=whole(4),
        out_specs=whole(3),
        compiler_params=params(28),
        cost_estimate=cheap(10),
        name="turn",
    )(*pieces)


def gram_kernel(p_ref, keep_ref, give_ref, blocks):
    at = 0
    for i in range(4):
        strip = tdot(p_ref[:, i * 128:i * 128 + 128], p_ref[:, i * 128:])
        for j in range(4 - i):
            blocks[at:at + 128, :] = strip[:, j * 128:j * 128 + 128]
            at += 128
    core = lax.axis_index("row") % 2
    keep_ref[...] = blocks[pl.ds(pl.multiple_of(core * 640, 128), 640), :]
    give_ref[...] = blocks[pl.ds(pl.multiple_of((1 - core) * 640, 128), 640), :]


def gram_share(rows):
    half = jax.ShapeDtypeStruct((640, 128), F32)
    return pl.pallas_call(
        gram_kernel,
        out_shape=(half, half),
        in_specs=whole(),
        out_specs=whole(2),
        scratch_shapes=[pltpu.VMEM((1280, 128), F32)],
        compiler_params=params(28),
        cost_estimate=cheap(10),
        name="gram",
    )(rows)


def swap(a, pairs):
    return lax.ppermute(a, "row", pairs)


def columns(first, i):
    return pl.ds(pl.multiple_of(first + i * TILE, TILE), TILE)


def fetch(hbm, buf, sems, first):
    def copy(i):
        return pltpu.make_async_copy(hbm.at[:, columns(first, i)], buf.at[i], sems.at[i])

    for i in range(buf.shape[0]):
        copy(i).start()
    return copy


def share_kernel(first, hi_ref, lo_ref, t_hbm, keep_ref, give_ref, buf, whole_share, sems):
    at_spot = spots(lax.axis_index("row"))
    copy = fetch(t_hbm, buf, sems, first)

    @pl.loop(0, buf.shape[0])
    def _(i):
        copy(i).wait()
        whole_share[...] = dot3((hi_ref[...], lo_ref[...]), split(buf[i]))
        for p in range(8):
            block = pl.ds(pl.multiple_of(at_spot[p] * 64, 64), 64)
            ref = (keep_ref, give_ref)[p // 4]
            ref[p % 4 * 64:p % 4 * 64 + 64, columns(0, i)] = whole_share[block, :]


def share(hi, lo, trailing, first, width):
    depth = trailing.shape[0]
    half = jax.ShapeDtypeStruct((256, width), F32)
    return pl.pallas_call(
        functools.partial(share_kernel, first),
        out_shape=(half, half),
        in_specs=whole(2) + [FAR],
        out_specs=whole(2),
        scratch_shapes=[
            pltpu.VMEM((width // TILE, depth, TILE), F32),
            pltpu.VMEM((512, TILE), F32),
            pltpu.SemaphoreType.DMA((width // TILE,)),
        ],
        compiler_params=params(28),
        cost_estimate=cheap(10),
        name="share",
    )(hi, lo, trailing)


def fold_kernel(k0, k1, g0, g1, keep_ref, give_ref):
    n = k0.shape[1]
    for cols, k, g in ((slice(0, n), k0, g0), (slice(n, 2 * n), k1, g1)):
        give_ref[:, cols] = k[128:, :] + g[128:, :]
        keep_ref[:, cols] = k[:128, :] + g[:128, :]


def fold(keeps, gots):
    out = jax.ShapeDtypeStruct((128, 2 * keeps[0].shape[1]), F32)
    return pl.pallas_call(
        fold_kernel,
        out_shape=(out, out),
        in_specs=whole(4),
        out_specs=whole(2),
        compiler_params=params(28),
        cost_estimate=cheap(),
        name="fold",
    )(*keeps, *gots)


def prepare_kernel(w0, w1, w2, w3, p_ref, r_ref, ihi_ref, ilo_ref, bhi_ref, blo_ref, inv):
    ri = lax.broadcasted_iota(jnp.int32, (128, 128), 0)
    ci = lax.broadcasted_iota(jnp.int32, (128, 128), 1)
    zero = jnp.zeros((128, 128), F32)
    for i, w in enumerate((w0, w1, w2, w3)):
        rows = slice(i * 128, i * 128 + 128)
        for j in range(4):
            cols = slice(j * 128, j * 128 + 128)
            if j < i:
                r_ref[rows, cols] = zero
            else:
                block = w[:, (j - i) * 128:(j - i) * 128 + 128]
                r_ref[rows, cols] = jnp.where(ri <= ci, block, 0.0) if j == i else block
            inv[rows, cols] = w[:, (4 - i + j) * 128:(5 - i + j) * 128] if j <= i else zero
    ihi_ref[...], ilo_ref[...] = split(inv[...])
    turned = split(jnp.transpose(inv[...]))
    for at in range(0, 1024, 256):
        rows = slice(at, at + 256)
        bhi_ref[rows, :], blo_ref[rows, :] = split(dot3(split(p_ref[rows, :]), turned))


def prepare(factors, rows):
    b = rows.shape[1]
    square, tall = (b, b), rows.shape
    return pl.pallas_call(
        prepare_kernel,
        out_shape=[jax.ShapeDtypeStruct(s, t) for s, t in ((square, F32), (square, BF16), (square, BF16), (tall, BF16), (tall, BF16))],
        in_specs=whole(5),
        out_specs=whole(5),
        scratch_shapes=[pltpu.VMEM(square, F32)],
        compiler_params=params(28),
        cost_estimate=cheap(),
        name="prepare",
    )(*factors, rows)


def finish_kernel(first, *refs):
    pieces, (ihi, ilo, bhi, blo, t_hbm) = refs[:4], refs[4:9]
    c_hbm, o_hbm, buf, total, cbuf, in_sems, c_sems, o_sems = refs[-8:]
    n = total.shape[0] // 2
    at_spot = spots(lax.axis_index("row"))
    copy = fetch(t_hbm, buf, in_sems, first)
    tall = buf.shape[1] // 2

    def c_copy(i):
        return pltpu.make_async_copy(cbuf.at[i], c_hbm.at[:, columns(first, i)], c_sems.at[i])

    def o_copy(i, r):
        rows = pl.ds(pl.multiple_of(r * tall, tall), tall)
        return pltpu.make_async_copy(buf.at[i, rows, :], o_hbm.at[rows, columns(first, i)], o_sems.at[2 * i + r])

    @pl.loop(0, buf.shape[0])
    def _(i):
        for p in range(8):
            at = pl.multiple_of(at_spot[p] * 64, 64)
            total[pl.ds(at, 64), :] = pieces[p // 2][p % 2 * 64:p % 2 * 64 + 64, columns(0, i)]
        high, low = split(total[...])
        for rows, depth in ((slice(0, n), n), (slice(n, 2 * n), 2 * n)):
            cbuf[i, rows, :] = dot3((ihi[rows, :depth], ilo[rows, :depth]), (high[:depth, :], low[:depth, :]))
        c_copy(i).start()
        c = split(cbuf[i])
        copy(i).wait()

        @pl.loop(0, 2)
        def _(r):
            rows = pl.ds(pl.multiple_of(r * tall, tall), tall)
            buf[i, rows, :] = buf[i, rows, :] - dot3((bhi[rows, :], blo[rows, :]), c)
            o_copy(i, r).start()

    @pl.loop(0, buf.shape[0])
    def _(i):
        c_copy(i).wait()
        o_copy(i, 0).wait()
        o_copy(i, 1).wait()


def finish(pieces, ihi, ilo, bhi, blo, trailing, first, done):
    depth, width = trailing.shape
    b = ihi.shape[0]
    tiles = pieces[0].shape[1] // TILE
    return pl.pallas_call(
        functools.partial(finish_kernel, first),
        out_shape=(jax.ShapeDtypeStruct((b, width), F32), jax.ShapeDtypeStruct((depth, width), F32)),
        in_specs=whole(8) + [FAR] * (1 + len(done)),
        out_specs=(FAR, FAR),
        scratch_shapes=[
            pltpu.VMEM((tiles, depth, TILE), F32),
            pltpu.VMEM((b, TILE), F32),
            pltpu.VMEM((tiles, b, TILE), F32),
            pltpu.SemaphoreType.DMA((tiles,)),
            pltpu.SemaphoreType.DMA((tiles,)),
            pltpu.SemaphoreType.DMA((2 * tiles,)),
        ],
        input_output_aliases={9 + i: i for i in range(len(done))},
        compiler_params=params(28),
        cost_estimate=cheap(),
        name="finish",
    )(*pieces, ihi, ilo, bhi, blo, trailing, *done)


def after(value, *others):
    return lax.optimization_barrier((value, others))[0]


def local(panel, trailing):
    rows, hi, lo = turn(gather_panel(panel))
    width = trailing.shape[1] // 2
    gram_keep, gram_give = gram_share(rows)
    gram_came = swap(gram_give, CORE)
    gram = gram_keep + gram_came
    came = swap(gram, ROW[0])
    first = share(after(hi, gram), lo, trailing, 0, width)
    gram = after(gram, first[0]) + came
    came = swap(gram, ROW[1])
    second = share(after(hi, gram, first[0]), lo, trailing, width, width)
    gram = gram + came
    second, gram = lax.optimization_barrier((second, gram))
    keep, give = fold((first[0], second[0]), [swap(g, CORE) for g in (first[1], second[1])])

    x_came = swap(give, ROW[0])
    packed = (gram, swap(gram, CORE))
    factors = [factor_rows(0, 4, [], packed)]
    factors.append(factor_rows(1, 4, factors, packed))
    keep, came, factors = lax.optimization_barrier((keep, x_came, factors))
    give, keep = keep[64:] + came[64:], keep[:64] + came[:64]
    came = swap(give, ROW[1])
    factors.append(factor_rows(2, 4, factors, packed))
    factors.append(factor_rows(3, 4, factors, packed))
    own, factors = lax.optimization_barrier((keep + came, factors))
    came = swap(own, ROW[1])
    r_factor, ihi, ilo, bhi, blo = prepare(factors, rows)
    own, came, ihi = lax.optimization_barrier((own, came, ihi))
    done = ()
    own = [jnp.concatenate([own[:, at:at + width], came[:, at:at + width]], axis=0) for at in (0, width)]
    came = [swap(own[0], ROW[0])]
    own[1] = after(own[1], came[0])
    came.append(swap(own[1], ROW[0]))
    own_across = [swap(p, CORE) for p in own]
    for c in (0, 1):
        pieces = [own[c], came[c], own_across[c], swap(came[c], CORE)]
        done = finish(pieces, ihi, ilo, bhi, blo, trailing, c * width, done)
        if c == 0:
            done, came = lax.optimization_barrier((done, came))
    return (r_factor, *done)


def solution(mesh):
    placed = (P(("row", "col"), None), P("row", "col"))
    return jax.shard_map(
        local,
        mesh=mesh,
        in_specs=placed,
        out_specs=(P(), P(None, "col"), P("row", "col")),
        check_vma=False,
    )
```

```python
import functools

import jax
import jax.numpy as jnp
from jax import lax
from jax.experimental import pallas as pl
from jax.experimental.pallas import tpu as pltpu
from jax.sharding import PartitionSpec as P

HIGHEST = lax.Precision.HIGHEST
BF16 = jnp.bfloat16
F32 = jnp.float32
GROUP = 32
TILE = 512


def near(i):
    return i ^ 1


def far(i):
    return 3 - i


PAIR = (near, far)
CORE = [(r, r ^ 1) for r in range(8)]
ROW = [[(x * 2 + c, PAIR[c ^ step](x) * 2 + c) for x in range(4) for c in (0, 1)] for step in (0, 1)]


def spots(row):
    core, x = row % 2, row // 2
    bits = ((x ^ (x // 2)) & 1, x // 2)
    out = []
    for half in (0, 1):
        owner = half ^ core
        one = jnp.where(owner == 0, bits[0], bits[1])
        two = jnp.where(owner == 0, bits[1], bits[0])
        out += [owner * 4 + (i ^ one) * 2 + (j ^ two) for i in (0, 1) for j in (0, 1)]
    return out


def places(core, col):
    out = []
    for q in (0, 1):
        place = [(col // 4, col % 4)]
        for step in range(4):
            flip = PAIR[(step % 2) ^ q]
            along_z = core == step // 2
            place = place + [(jnp.where(along_z, y, flip(y)), jnp.where(along_z, flip(z), z)) for y, z in place]
        out += [y * 4 + z for y, z in place]
    return out


def tdot(a, b, precision=HIGHEST):
    return lax.dot_general(a, b, (((0,), (0,)), ((), ())), precision=precision, preferred_element_type=F32)


def spread(v, s):
    return jnp.broadcast_to(v[s:s + 1, :], (8, 128))


def eliminate(slab, off, g):
    nt = g // 8
    width = slab.shape[1] // 128
    sub = lax.broadcasted_iota(jnp.int32, (8, 128), 0)
    rows = [[slab[8 * t:8 * t + 8, 128 * w:128 * w + 128] for w in range(width)] for t in range(nt)]
    cols = [
        [jnp.broadcast_to(rows[t][0][:, off + k:off + k + 1], (8, 128)) if t >= k // 8 else None for t in range(nt)]
        for k in range(g)
    ]
    scale = [None] * nt
    for j in range(g):
        tj, sj = divmod(j, 8)
        d = spread(cols[j][tj], sj)
        inv = 1.0 / d
        root = lax.rsqrt(d)
        scale[tj] = root if sj == 0 else jnp.where(sub >= sj, root, scale[tj])
        f = [None if t < tj else cols[j][t] * inv for t in range(nt)]
        for k in range(j + 1, g):
            a = spread(cols[j][k // 8], k % 8)
            for t in range(k // 8, nt):
                cols[k][t] = cols[k][t] - f[t] * a
        f[tj] = jnp.where(sub > sj, f[tj], 0.0)
        for w in range(width):
            p = spread(rows[tj][w], sj)
            for t in range(tj, nt):
                if t > tj or sj < 7:
                    rows[t][w] = rows[t][w] - f[t] * p
    return jnp.concatenate(
        [jnp.concatenate([rows[t][w] * scale[t] for w in range(width)], axis=1) for t in range(nt)], axis=0
    )


def params(mib):
    return pltpu.CompilerParams(vmem_limit_bytes=mib << 20)


def cheap(times=1):
    return pl.CostEstimate(flops=times * 3 * 10 ** 8, bytes_accessed=times * 10 ** 6, transcendentals=0)


def whole(n=1):
    return [pl.BlockSpec(memory_space=pltpu.VMEM)] * n


FAR = pl.BlockSpec(memory_space=pltpu.HBM)


def split(a):
    high = a.astype(BF16)
    return high, (a - high.astype(F32)).astype(BF16)


def dot(a, b):
    return jnp.dot(a, b, preferred_element_type=F32)


def dot3(a, b):
    return dot(a[0], b[0]) + (dot(a[0], b[1]) + dot(a[1], b[0]))


def factor_kernel(k, nb, *refs):
    earlier, (own, other, w, m) = refs[:k], refs[k:]
    core = lax.axis_index("row") % 2
    first = sum(nb - i for i in range(k))
    for j in range(nb - k):
        half, at = divmod(first + j, own.shape[0] // 128)
        rows = slice(at * 128, at * 128 + 128)
        m[:, j * 128:j * 128 + 128] = jnp.where(core == half, own[rows, :], other[rows, :])
    if k:
        m[:, (nb - k) * 128:nb * 128] = jnp.zeros((128, k * 128), F32)
    ri = lax.broadcasted_iota(jnp.int32, (128, 128), 0)
    ci = lax.broadcasted_iota(jnp.int32, (128, 128), 1)
    m[:, nb * 128:] = jnp.where(ri == ci, 1.0, 0.0)
    for i in range(k):
        at = (k - i) * 128
        known = earlier[i][:, at:]
        width = known.shape[1]
        m[:, :width] = m[:, :width] - tdot(earlier[i][:, at:at + 128], known)
    for q in range(128 // GROUP):
        lo, hi = q * GROUP, (q + 1) * GROUP
        slab = m[lo:hi, :]
        if q:
            slab = slab - tdot(w[0:lo, lo:hi], w[0:lo, :])
        w[lo:hi, :] = eliminate(slab, lo, GROUP)


def factor_rows(k, nb, earlier, packed):
    window = (nb + 1) * 128
    return pl.pallas_call(
        functools.partial(factor_kernel, k, nb),
        out_shape=jax.ShapeDtypeStruct((128, window), F32),
        in_specs=whole(k + 2),
        out_specs=whole()[0],
        scratch_shapes=[pltpu.VMEM((128, window), F32)],
        compiler_params=params(28),
        cost_estimate=cheap(),
        name="factor",
    )(*earlier, *packed)


def gather_pairs(q, step):
    out = []
    for x in range(4):
        for c in (0, 1):
            for y in range(4):
                for z in range(4):
                    flip = PAIR[(step % 2) ^ q]
                    to = (y, flip(z)) if (step // 2) ^ c == 0 else (flip(y), z)
                    out.append(((x * 2 + c) * 16 + y * 4 + z, (x * 2 + c) * 16 + to[0] * 4 + to[1]))
    return out


def gather_panel(panel):
    n = panel.shape[1] // 2
    pieces = [[panel[:, :n]], [panel[:, n:]]]
    for step in range(4):
        held = [p[0] if len(p) == 1 else jnp.concatenate(p, axis=0) for p in pieces]
        pieces = [[h, lax.ppermute(h, ("row", "col"), gather_pairs(q, step))] for q, h in enumerate(held)]
    return pieces[0] + pieces[1]


def turn_kernel(*refs):
    pieces, (o_ref, hi_ref, lo_ref) = refs[:4], refs[4:]
    order = places(lax.axis_index("row") % 2, lax.axis_index("col"))
    for i, ref in enumerate(pieces):
        q = i // 2
        for p in range(8):
            at = pl.multiple_of(order[i * 8 + p] * 64, 64)
            o_ref[pl.ds(at, 64), q * 256:q * 256 + 256] = ref[p * 64:p * 64 + 64, :]
    for j in range(0, 1024, 128):
        hi_ref[:, j:j + 128], lo_ref[:, j:j + 128] = split(jnp.transpose(o_ref[j:j + 128, :]))


def turn(pieces):
    depth, b = pieces[0].shape[0] * 2, pieces[0].shape[1] * 2
    out = jax.ShapeDtypeStruct((b, depth), BF16)
    return pl.pallas_call(
        turn_kernel,
        out_shape=(jax.ShapeDtypeStruct((depth, b), F32), out, out),
        in_specs=whole(4),
        out_specs=whole(3),
        compiler_params=params(28),
        cost_estimate=cheap(10),
        name="turn",
    )(*pieces)


def gram_kernel(p_ref, keep_ref, give_ref, blocks):
    at = 0
    for i in range(4):
        strip = tdot(p_ref[:, i * 128:i * 128 + 128], p_ref[:, i * 128:])
        for j in range(4 - i):
            blocks[at:at + 128, :] = strip[:, j * 128:j * 128 + 128]
            at += 128
    core = lax.axis_index("row") % 2
    keep_ref[...] = blocks[pl.ds(pl.multiple_of(core * 640, 128), 640), :]
    give_ref[...] = blocks[pl.ds(pl.multiple_of((1 - core) * 640, 128), 640), :]


def gram_share(rows):
    half = jax.ShapeDtypeStruct((640, 128), F32)
    return pl.pallas_call(
        gram_kernel,
        out_shape=(half, half),
        in_specs=whole(),
        out_specs=whole(2),
        scratch_shapes=[pltpu.VMEM((1280, 128), F32)],
        compiler_params=params(28),
        cost_estimate=cheap(10),
        name="gram",
    )(rows)


def swap(a, pairs):
    return lax.ppermute(a, "row", pairs)


def columns(first, i):
    return pl.ds(pl.multiple_of(first + i * TILE, TILE), TILE)


def fetch(hbm, buf, sems, first):
    def copy(i):
        return pltpu.make_async_copy(hbm.at[:, columns(first, i)], buf.at[i], sems.at[i])

    for i in range(buf.shape[0]):
        copy(i).start()
    return copy


def share_kernel(first, hi_ref, lo_ref, t_hbm, keep_ref, give_ref, buf, whole_share, sems):
    at_spot = spots(lax.axis_index("row"))
    copy = fetch(t_hbm, buf, sems, first)

    @pl.loop(0, buf.shape[0])
    def _(i):
        copy(i).wait()
        whole_share[...] = dot3((hi_ref[...], lo_ref[...]), split(buf[i]))
        for p in range(8):
            block = pl.ds(pl.multiple_of(at_spot[p] * 64, 64), 64)
            ref = (keep_ref, give_ref)[p // 4]
            ref[p % 4 * 64:p % 4 * 64 + 64, columns(0, i)] = whole_share[block, :]


def share(hi, lo, trailing, first, width):
    depth = trailing.shape[0]
    half = jax.ShapeDtypeStruct((256, width), F32)
    return pl.pallas_call(
        functools.partial(share_kernel, first),
        out_shape=(half, half),
        in_specs=whole(2) + [FAR],
        out_specs=whole(2),
        scratch_shapes=[
            pltpu.VMEM((width // TILE, depth, TILE), F32),
            pltpu.VMEM((512, TILE), F32),
            pltpu.SemaphoreType.DMA((width // TILE,)),
        ],
        compiler_params=params(28),
        cost_estimate=cheap(10),
        name="share",
    )(hi, lo, trailing)


def prepare_kernel(w0, w1, w2, w3, p_ref, r_ref, ihi_ref, ilo_ref, bhi_ref, blo_ref, inv):
    ri = lax.broadcasted_iota(jnp.int32, (128, 128), 0)
    ci = lax.broadcasted_iota(jnp.int32, (128, 128), 1)
    zero = jnp.zeros((128, 128), F32)
    for i, w in enumerate((w0, w1, w2, w3)):
        rows = slice(i * 128, i * 128 + 128)
        for j in range(4):
            cols = slice(j * 128, j * 128 + 128)
            if j < i:
                r_ref[rows, cols] = zero
            else:
                block = w[:, (j - i) * 128:(j - i) * 128 + 128]
                r_ref[rows, cols] = jnp.where(ri <= ci, block, 0.0) if j == i else block
            inv[rows, cols] = w[:, (4 - i + j) * 128:(5 - i + j) * 128] if j <= i else zero
    ihi_ref[...], ilo_ref[...] = split(inv[...])
    turned = split(jnp.transpose(inv[...]))
    for at in range(0, 1024, 256):
        rows = slice(at, at + 256)
        bhi_ref[rows, :], blo_ref[rows, :] = split(dot3(split(p_ref[rows, :]), turned))


def prepare(factors, rows):
    b = rows.shape[1]
    square, tall = (b, b), rows.shape
    return pl.pallas_call(
        prepare_kernel,
        out_shape=[jax.ShapeDtypeStruct(s, t) for s, t in ((square, F32), (square, BF16), (square, BF16), (tall, BF16), (tall, BF16))],
        in_specs=whole(5),
        out_specs=whole(5),
        scratch_shapes=[pltpu.VMEM(square, F32)],
        compiler_params=params(28),
        cost_estimate=cheap(),
        name="prepare",
    )(*factors, rows)


def finish_kernel(first, *refs):
    pieces, (ihi, ilo, bhi, blo, t_hbm) = refs[:4], refs[4:9]
    c_hbm, o_hbm, buf, total, cbuf, in_sems, c_sems, o_sems = refs[-8:]
    n = total.shape[0] // 2
    at_spot = spots(lax.axis_index("row"))
    copy = fetch(t_hbm, buf, in_sems, first)
    tall = buf.shape[1] // 2

    def c_copy(i):
        return pltpu.make_async_copy(cbuf.at[i], c_hbm.at[:, columns(first, i)], c_sems.at[i])

    def o_copy(i, r):
        rows = pl.ds(pl.multiple_of(r * tall, tall), tall)
        return pltpu.make_async_copy(buf.at[i, rows, :], o_hbm.at[rows, columns(first, i)], o_sems.at[2 * i + r])

    @pl.loop(0, buf.shape[0])
    def _(i):
        for p in range(8):
            at = pl.multiple_of(at_spot[p] * 64, 64)
            total[pl.ds(at, 64), :] = pieces[p // 2][p % 2 * 64:p % 2 * 64 + 64, columns(0, i)]
        high, low = split(total[...])
        for rows, depth in ((slice(0, n), n), (slice(n, 2 * n), 2 * n)):
            cbuf[i, rows, :] = dot3((ihi[rows, :depth], ilo[rows, :depth]), (high[:depth, :], low[:depth, :]))
        c_copy(i).start()
        c = split(cbuf[i])
        copy(i).wait()

        @pl.loop(0, 2)
        def _(r):
            rows = pl.ds(pl.multiple_of(r * tall, tall), tall)
            buf[i, rows, :] = buf[i, rows, :] - dot3((bhi[rows, :], blo[rows, :]), c)
            o_copy(i, r).start()

    @pl.loop(0, buf.shape[0])
    def _(i):
        c_copy(i).wait()
        o_copy(i, 0).wait()
        o_copy(i, 1).wait()


def finish(pieces, ihi, ilo, bhi, blo, trailing, first, done):
    depth, width = trailing.shape
    b = ihi.shape[0]
    tiles = pieces[0].shape[1] // TILE
    return pl.pallas_call(
        functools.partial(finish_kernel, first),
        out_shape=(jax.ShapeDtypeStruct((b, width), F32), jax.ShapeDtypeStruct((depth, width), F32)),
        in_specs=whole(8) + [FAR] * (1 + len(done)),
        out_specs=(FAR, FAR),
        scratch_shapes=[
            pltpu.VMEM((tiles, depth, TILE), F32),
            pltpu.VMEM((b, TILE), F32),
            pltpu.VMEM((tiles, b, TILE), F32),
            pltpu.SemaphoreType.DMA((tiles,)),
            pltpu.SemaphoreType.DMA((tiles,)),
            pltpu.SemaphoreType.DMA((2 * tiles,)),
        ],
        input_output_aliases={9 + i: i for i in range(len(done))},
        compiler_params=params(28),
        cost_estimate=cheap(),
        name="finish",
    )(*pieces, ihi, ilo, bhi, blo, trailing, *done)


def after(value, *others):
    return lax.optimization_barrier((value, others))[0]


def local(panel, trailing):
    rows, hi, lo = turn(gather_panel(panel))
    width = trailing.shape[1] // 2
    gram_keep, gram_give = gram_share(rows)
    gram_came = swap(gram_give, CORE)
    gram = gram_keep + gram_came
    came = swap(gram, ROW[0])
    first = share(after(hi, gram), lo, trailing, 0, width)
    gram = after(gram, first[0]) + came
    came = swap(gram, ROW[1])
    second = share(after(hi, gram, first[0]), lo, trailing, width, width)
    gram = gram + came
    second, gram = lax.optimization_barrier((second, gram))

    keeps, gives = [], []
    for keep, give in (first, second):
        got = swap(give, CORE)
        gives.append(keep[128:] + got[128:])
        keeps.append(keep[:128] + got[:128])
    came = [swap(g, ROW[0]) for g in gives]
    packed = (gram, swap(gram, CORE))
    factors = []
    for c in (0, 1):
        factors.append(factor_rows(c, 4, factors, packed))
        came[c], keeps[c], factors[-1] = lax.optimization_barrier((came[c], keeps[c], factors[-1]))
        give, keeps[c] = keeps[c][64:] + came[c][64:], keeps[c][:64] + came[c][:64]
        came[c] = swap(give, ROW[1])
    own = []
    for c in (0, 1):
        factors.append(factor_rows(2 + c, 4, factors, packed))
        came[c], keeps[c], factors[-1] = lax.optimization_barrier((came[c], keeps[c], factors[-1]))
        own.append(keeps[c] + came[c])
        came[c] = swap(own[c], ROW[1])
    r_factor, ihi, ilo, bhi, blo = prepare(factors, after(rows, own[1]))
    own[0], came[0], ihi = lax.optimization_barrier((own[0], came[0], ihi))
    own = [jnp.concatenate(p, axis=0) for p in zip(own, came)]
    came = [swap(own[0], ROW[0])]
    own[1] = after(own[1], came[0])
    came.append(swap(own[1], ROW[0]))
    own_across = [swap(p, CORE) for p in own]
    done = ()
    for c in (0, 1):
        pieces = [own[c], came[c], own_across[c], swap(came[c], CORE)]
        done = finish(pieces, ihi, ilo, bhi, blo, trailing, c * width, done)
        if c == 0:
            done, came = lax.optimization_barrier((done, came))
    return (r_factor, *done)


def solution(mesh):
    placed = (P(("row", "col"), None), P("row", "col"))
    return jax.shard_map(
        local,
        mesh=mesh,
        in_specs=placed,
        out_specs=(P(), P(None, "col"), P("row", "col")),
        check_vma=False,
    )
```

```python
import functools

import jax
import jax.numpy as jnp
from jax import lax
from jax.experimental import pallas as pl
from jax.experimental.pallas import tpu as pltpu
from jax.sharding import PartitionSpec as P

HIGHEST = lax.Precision.HIGHEST
BF16 = jnp.bfloat16
F32 = jnp.float32
GROUP = 32
TILE = 512


def near(i):
    return i ^ 1


def far(i):
    return 3 - i


PAIR = (near, far)
CORE = [(r, r ^ 1) for r in range(8)]
ROW = [[(x * 2 + c, PAIR[c ^ step](x) * 2 + c) for x in range(4) for c in (0, 1)] for step in (0, 1)]


def spots(row):
    core, x = row % 2, row // 2
    bits = ((x ^ (x // 2)) & 1, x // 2)
    out = []
    for half in (0, 1):
        owner = half ^ core
        one = jnp.where(owner == 0, bits[0], bits[1])
        two = jnp.where(owner == 0, bits[1], bits[0])
        out += [owner * 4 + (i ^ one) * 2 + (j ^ two) for i in (0, 1) for j in (0, 1)]
    return out


def places(core, col):
    out = []
    for q in (0, 1):
        place = [(col // 4, col % 4)]
        for step in range(4):
            flip = PAIR[(step % 2) ^ q]
            along_z = core == step // 2
            place = place + [(jnp.where(along_z, y, flip(y)), jnp.where(along_z, flip(z), z)) for y, z in place]
        out += [y * 4 + z for y, z in place]
    return out


def tdot(a, b, precision=HIGHEST):
    return lax.dot_general(a, b, (((0,), (0,)), ((), ())), precision=precision, preferred_element_type=F32)


def spread(v, s):
    return jnp.broadcast_to(v[s:s + 1, :], (8, 128))


def eliminate(slab, off, g):
    nt = g // 8
    width = slab.shape[1] // 128
    sub = lax.broadcasted_iota(jnp.int32, (8, 128), 0)
    rows = [[slab[8 * t:8 * t + 8, 128 * w:128 * w + 128] for w in range(width)] for t in range(nt)]
    cols = [
        [jnp.broadcast_to(rows[t][0][:, off + k:off + k + 1], (8, 128)) if t >= k // 8 else None for t in range(nt)]
        for k in range(g)
    ]
    scale = [None] * nt
    for j in range(g):
        tj, sj = divmod(j, 8)
        d = spread(cols[j][tj], sj)
        inv = 1.0 / d
        root = lax.rsqrt(d)
        scale[tj] = root if sj == 0 else jnp.where(sub >= sj, root, scale[tj])
        f = [None if t < tj else cols[j][t] * inv for t in range(nt)]
        for k in range(j + 1, g):
            a = spread(cols[j][k // 8], k % 8)
            for t in range(k // 8, nt):
                cols[k][t] = cols[k][t] - f[t] * a
        f[tj] = jnp.where(sub > sj, f[tj], 0.0)
        for w in range(width):
            p = spread(rows[tj][w], sj)
            for t in range(tj, nt):
                if t > tj or sj < 7:
                    rows[t][w] = rows[t][w] - f[t] * p
    return jnp.concatenate(
        [jnp.concatenate([rows[t][w] * scale[t] for w in range(width)], axis=1) for t in range(nt)], axis=0
    )


def params(mib):
    return pltpu.CompilerParams(vmem_limit_bytes=mib << 20)


def cheap(times=1):
    return pl.CostEstimate(flops=times * 3 * 10 ** 8, bytes_accessed=times * 10 ** 6, transcendentals=0)


def whole(n=1):
    return [pl.BlockSpec(memory_space=pltpu.VMEM)] * n


FAR = pl.BlockSpec(memory_space=pltpu.HBM)


def split(a):
    high = a.astype(BF16)
    return high, (a - high.astype(F32)).astype(BF16)


def dot(a, b):
    return jnp.dot(a, b, preferred_element_type=F32)


def dot3(a, b):
    return dot(a[0], b[0]) + (dot(a[0], b[1]) + dot(a[1], b[0]))


def factor_kernel(k, nb, *refs):
    earlier, (own, other, w, m) = refs[:k], refs[k:]
    core = lax.axis_index("row") % 2
    first = sum(nb - i for i in range(k))
    for j in range(nb - k):
        half, at = divmod(first + j, own.shape[0] // 128)
        rows = slice(at * 128, at * 128 + 128)
        m[:, j * 128:j * 128 + 128] = jnp.where(core == half, own[rows, :], other[rows, :])
    if k:
        m[:, (nb - k) * 128:nb * 128] = jnp.zeros((128, k * 128), F32)
    ri = lax.broadcasted_iota(jnp.int32, (128, 128), 0)
    ci = lax.broadcasted_iota(jnp.int32, (128, 128), 1)
    m[:, nb * 128:] = jnp.where(ri == ci, 1.0, 0.0)
    for i in range(k):
        at = (k - i) * 128
        known = earlier[i][:, at:]
        width = known.shape[1]
        m[:, :width] = m[:, :width] - tdot(earlier[i][:, at:at + 128], known)
    for q in range(128 // GROUP):
        lo, hi = q * GROUP, (q + 1) * GROUP
        slab = m[lo:hi, :]
        if q:
            slab = slab - tdot(w[0:lo, lo:hi], w[0:lo, :])
        w[lo:hi, :] = eliminate(slab, lo, GROUP)


def factor_rows(k, nb, earlier, packed):
    window = (nb + 1) * 128
    return pl.pallas_call(
        functools.partial(factor_kernel, k, nb),
        out_shape=jax.ShapeDtypeStruct((128, window), F32),
        in_specs=whole(k + 2),
        out_specs=whole()[0],
        scratch_shapes=[pltpu.VMEM((128, window), F32)],
        compiler_params=params(28),
        cost_estimate=cheap(),
        name="factor",
    )(*earlier, *packed)


def gather_pairs(q, step):
    out = []
    for x in range(4):
        for c in (0, 1):
            for y in range(4):
                for z in range(4):
                    flip = PAIR[(step % 2) ^ q]
                    to = (y, flip(z)) if (step // 2) ^ c == 0 else (flip(y), z)
                    out.append(((x * 2 + c) * 16 + y * 4 + z, (x * 2 + c) * 16 + to[0] * 4 + to[1]))
    return out


def gather_panel(panel):
    n = panel.shape[1] // 2
    pieces = [[panel[:, :n]], [panel[:, n:]]]
    for step in range(4):
        held = [p[0] if len(p) == 1 else jnp.concatenate(p, axis=0) for p in pieces]
        pieces = [[h, lax.ppermute(h, ("row", "col"), gather_pairs(q, step))] for q, h in enumerate(held)]
    return pieces[0] + pieces[1]


def turn_kernel(*refs):
    pieces, (o_ref, hi_ref, lo_ref) = refs[:4], refs[4:]
    order = places(lax.axis_index("row") % 2, lax.axis_index("col"))
    for i, ref in enumerate(pieces):
        q = i // 2
        for p in range(8):
            at = pl.multiple_of(order[i * 8 + p] * 64, 64)
            o_ref[pl.ds(at, 64), q * 256:q * 256 + 256] = ref[p * 64:p * 64 + 64, :]
    for j in range(0, 1024, 128):
        hi_ref[:, j:j + 128], lo_ref[:, j:j + 128] = split(jnp.transpose(o_ref[j:j + 128, :]))


def turn(pieces):
    depth, b = pieces[0].shape[0] * 2, pieces[0].shape[1] * 2
    out = jax.ShapeDtypeStruct((b, depth), BF16)
    return pl.pallas_call(
        turn_kernel,
        out_shape=(jax.ShapeDtypeStruct((depth, b), F32), out, out),
        in_specs=whole(4),
        out_specs=whole(3),
        compiler_params=params(28),
        cost_estimate=cheap(10),
        name="turn",
    )(*pieces)


def gram_kernel(p_ref, keep_ref, give_ref, blocks):
    at = 0
    for i in range(4):
        strip = tdot(p_ref[:, i * 128:i * 128 + 128], p_ref[:, i * 128:])
        for j in range(4 - i):
            blocks[at:at + 128, :] = strip[:, j * 128:j * 128 + 128]
            at += 128
    core = lax.axis_index("row") % 2
    keep_ref[...] = blocks[pl.ds(pl.multiple_of(core * 640, 128), 640), :]
    give_ref[...] = blocks[pl.ds(pl.multiple_of((1 - core) * 640, 128), 640), :]


def gram_share(rows):
    half = jax.ShapeDtypeStruct((640, 128), F32)
    return pl.pallas_call(
        gram_kernel,
        out_shape=(half, half),
        in_specs=whole(),
        out_specs=whole(2),
        scratch_shapes=[pltpu.VMEM((1280, 128), F32)],
        compiler_params=params(28),
        cost_estimate=cheap(10),
        name="gram",
    )(rows)


def swap(a, pairs):
    return lax.ppermute(a, "row", pairs)


def columns(first, i):
    return pl.ds(pl.multiple_of(first + i * TILE, TILE), TILE)


def fetch(hbm, buf, sems, first):
    def copy(i):
        return pltpu.make_async_copy(hbm.at[:, columns(first, i)], buf.at[i], sems.at[i])

    for i in range(buf.shape[0]):
        copy(i).start()
    return copy


def share_kernel(first, hi_ref, lo_ref, t_hbm, keep_ref, give_ref, buf, whole_share, sems):
    at_spot = spots(lax.axis_index("row"))
    copy = fetch(t_hbm, buf, sems, first)

    @pl.loop(0, buf.shape[0])
    def _(i):
        copy(i).wait()
        whole_share[...] = dot3((hi_ref[...], lo_ref[...]), split(buf[i]))
        for p in range(8):
            block = pl.ds(pl.multiple_of(at_spot[p] * 64, 64), 64)
            ref = (keep_ref, give_ref)[p // 4]
            ref[p % 4 * 64:p % 4 * 64 + 64, columns(0, i)] = whole_share[block, :]


def share(hi, lo, trailing, first, width):
    depth = trailing.shape[0]
    half = jax.ShapeDtypeStruct((256, width), F32)
    return pl.pallas_call(
        functools.partial(share_kernel, first),
        out_shape=(half, half),
        in_specs=whole(2) + [FAR],
        out_specs=whole(2),
        scratch_shapes=[
            pltpu.VMEM((width // TILE, depth, TILE), F32),
            pltpu.VMEM((512, TILE), F32),
            pltpu.SemaphoreType.DMA((width // TILE,)),
        ],
        compiler_params=params(28),
        cost_estimate=cheap(10),
        name="share",
    )(hi, lo, trailing)


def prepare_kernel(w0, w1, w2, w3, p_ref, r_ref, ihi_ref, ilo_ref, bhi_ref, blo_ref, inv):
    ri = lax.broadcasted_iota(jnp.int32, (128, 128), 0)
    ci = lax.broadcasted_iota(jnp.int32, (128, 128), 1)
    zero = jnp.zeros((128, 128), F32)
    for i, w in enumerate((w0, w1, w2, w3)):
        rows = slice(i * 128, i * 128 + 128)
        for j in range(4):
            cols = slice(j * 128, j * 128 + 128)
            if j < i:
                r_ref[rows, cols] = zero
            else:
                block = w[:, (j - i) * 128:(j - i) * 128 + 128]
                r_ref[rows, cols] = jnp.where(ri <= ci, block, 0.0) if j == i else block
            inv[rows, cols] = w[:, (4 - i + j) * 128:(5 - i + j) * 128] if j <= i else zero
    ihi_ref[...], ilo_ref[...] = split(inv[...])
    turned = split(jnp.transpose(inv[...]))
    for at in range(0, 1024, 256):
        rows = slice(at, at + 256)
        bhi_ref[rows, :], blo_ref[rows, :] = split(dot3(split(p_ref[rows, :]), turned))


def prepare(factors, rows):
    b = rows.shape[1]
    square, tall = (b, b), rows.shape
    return pl.pallas_call(
        prepare_kernel,
        out_shape=[jax.ShapeDtypeStruct(s, t) for s, t in ((square, F32), (square, BF16), (square, BF16), (tall, BF16), (tall, BF16))],
        in_specs=whole(5),
        out_specs=whole(5),
        scratch_shapes=[pltpu.VMEM(square, F32)],
        compiler_params=params(28),
        cost_estimate=cheap(),
        name="prepare",
    )(*factors, rows)


def finish_kernel(first, *refs):
    pieces, (ihi, ilo, bhi, blo, t_hbm) = refs[:4], refs[4:9]
    c_hbm, o_hbm, buf, total, cbuf, in_sems, c_sems, o_sems = refs[-8:]
    n = total.shape[0] // 2
    at_spot = spots(lax.axis_index("row"))
    copy = fetch(t_hbm, buf, in_sems, first)
    tall = buf.shape[1] // 2

    def c_copy(i):
        return pltpu.make_async_copy(cbuf.at[i], c_hbm.at[:, columns(first, i)], c_sems.at[i])

    def o_copy(i, r):
        rows = pl.ds(pl.multiple_of(r * tall, tall), tall)
        return pltpu.make_async_copy(buf.at[i, rows, :], o_hbm.at[rows, columns(first, i)], o_sems.at[2 * i + r])

    @pl.loop(0, buf.shape[0])
    def _(i):
        for p in range(8):
            at = pl.multiple_of(at_spot[p] * 64, 64)
            total[pl.ds(at, 64), :] = pieces[p // 2][p % 2 * 64:p % 2 * 64 + 64, columns(0, i)]
        high, low = split(total[...])
        for rows, depth in ((slice(0, n), n), (slice(n, 2 * n), 2 * n)):
            cbuf[i, rows, :] = dot3((ihi[rows, :depth], ilo[rows, :depth]), (high[:depth, :], low[:depth, :]))
        c_copy(i).start()
        c = split(cbuf[i])
        copy(i).wait()

        @pl.loop(0, 2)
        def _(r):
            rows = pl.ds(pl.multiple_of(r * tall, tall), tall)
            buf[i, rows, :] = buf[i, rows, :] - dot3((bhi[rows, :], blo[rows, :]), c)
            o_copy(i, r).start()

    @pl.loop(0, buf.shape[0])
    def _(i):
        c_copy(i).wait()
        o_copy(i, 0).wait()
        o_copy(i, 1).wait()


def finish(pieces, ihi, ilo, bhi, blo, trailing, first, done):
    depth, width = trailing.shape
    b = ihi.shape[0]
    tiles = pieces[0].shape[1] // TILE
    return pl.pallas_call(
        functools.partial(finish_kernel, first),
        out_shape=(jax.ShapeDtypeStruct((b, width), F32), jax.ShapeDtypeStruct((depth, width), F32)),
        in_specs=whole(8) + [FAR] * (1 + len(done)),
        out_specs=(FAR, FAR),
        scratch_shapes=[
            pltpu.VMEM((tiles, depth, TILE), F32),
            pltpu.VMEM((b, TILE), F32),
            pltpu.VMEM((tiles, b, TILE), F32),
            pltpu.SemaphoreType.DMA((tiles,)),
            pltpu.SemaphoreType.DMA((tiles,)),
            pltpu.SemaphoreType.DMA((2 * tiles,)),
        ],
        input_output_aliases={9 + i: i for i in range(len(done))},
        compiler_params=params(28),
        cost_estimate=cheap(),
        name="finish",
    )(*pieces, ihi, ilo, bhi, blo, trailing, *done)


def after(value, *others):
    return lax.optimization_barrier((value, others))[0]


def local(panel, trailing):
    rows, hi, lo = turn(gather_panel(panel))
    width = trailing.shape[1] // 2
    gram_keep, gram_give = gram_share(rows)
    gram_came = swap(gram_give, CORE)
    gram = gram_keep + gram_came
    came = swap(gram, ROW[0])
    first = share(after(hi, gram), lo, trailing, 0, width)
    gram = after(gram, first[0]) + came
    came = swap(gram, ROW[1])
    second = share(after(hi, gram, first[0]), lo, trailing, width, width)
    gram = gram + came
    second, gram = lax.optimization_barrier((second, gram))

    keeps, gives = [], []
    for keep, give in (first, second):
        got = swap(give, CORE)
        gives.append(keep[128:] + got[128:])
        keeps.append(keep[:128] + got[:128])
    came = [swap(g, ROW[0]) for g in gives]
    packed = (gram, swap(gram, CORE))
    factors = []
    for c in (0, 1):
        factors.append(factor_rows(c, 4, factors, packed))
        came[c], keeps[c], factors[-1] = lax.optimization_barrier((came[c], keeps[c], factors[-1]))
        give, keeps[c] = keeps[c][64:] + came[c][64:], keeps[c][:64] + came[c][:64]
        came[c] = swap(give, ROW[1])
    own = []
    for c in (0, 1):
        factors.append(factor_rows(2 + c, 4, factors, packed))
        came[c], keeps[c], factors[-1] = lax.optimization_barrier((came[c], keeps[c], factors[-1]))
        own.append(keeps[c] + came[c])
        came[c] = swap(own[c], ROW[1])
    r_factor, ihi, ilo, bhi, blo = prepare(factors, after(rows, own[1]))
    own, came, ihi = lax.optimization_barrier((own, came, ihi))
    own = [jnp.concatenate(p, axis=0) for p in zip(own, came)]
    came = [swap(own[0], ROW[0])]
    own[1] = after(own[1], came[0])
    came.append(swap(own[1], ROW[0]))
    own_across = [swap(p, CORE) for p in own]
    done = ()
    for c in (0, 1):
        pieces = [own[c], came[c], own_across[c], swap(came[c], CORE)]
        done = finish(pieces, ihi, ilo, bhi, blo, trailing, c * width, done)
        if c == 0:
            done, came = lax.optimization_barrier((done, came))
    return (r_factor, *done)


def solution(mesh):
    placed = (P(("row", "col"), None), P("row", "col"))
    return jax.shard_map(
        local,
        mesh=mesh,
        in_specs=placed,
        out_specs=(P(), P(None, "col"), P("row", "col")),
        check_vma=False,
    )
```

```python
import functools

import jax
import jax.numpy as jnp
from jax import lax
from jax.experimental import pallas as pl
from jax.experimental.pallas import tpu as pltpu
from jax.sharding import PartitionSpec as P

HIGHEST = lax.Precision.HIGHEST
BF16 = jnp.bfloat16
F32 = jnp.float32
GROUP = 32
TILE = 512


def near(i):
    return i ^ 1


def far(i):
    return 3 - i


PAIR = (near, far)
CORE = [(r, r ^ 1) for r in range(8)]
ROW = [[(x * 2 + c, PAIR[c ^ step](x) * 2 + c) for x in range(4) for c in (0, 1)] for step in (0, 1)]


def spots(row):
    core, x = row % 2, row // 2
    bits = ((x ^ (x // 2)) & 1, x // 2)
    out = []
    for half in (0, 1):
        owner = half ^ core
        one = jnp.where(owner == 0, bits[0], bits[1])
        two = jnp.where(owner == 0, bits[1], bits[0])
        out += [owner * 4 + (i ^ one) * 2 + (j ^ two) for i in (0, 1) for j in (0, 1)]
    return out


def places(core, col):
    out = []
    for q in (0, 1):
        place = [(col // 4, col % 4)]
        for step in range(4):
            flip = PAIR[(step % 2) ^ q]
            along_z = core == step // 2
            place = place + [(jnp.where(along_z, y, flip(y)), jnp.where(along_z, flip(z), z)) for y, z in place]
        out += [y * 4 + z for y, z in place]
    return out


def tdot(a, b, precision=HIGHEST):
    return lax.dot_general(a, b, (((0,), (0,)), ((), ())), precision=precision, preferred_element_type=F32)


def spread(v, s):
    return jnp.broadcast_to(v[s:s + 1, :], (8, 128))


def eliminate(slab, off, g):
    nt = g // 8
    width = slab.shape[1] // 128
    sub = lax.broadcasted_iota(jnp.int32, (8, 128), 0)
    rows = [[slab[8 * t:8 * t + 8, 128 * w:128 * w + 128] for w in range(width)] for t in range(nt)]
    cols = [
        [jnp.broadcast_to(rows[t][0][:, off + k:off + k + 1], (8, 128)) if t >= k // 8 else None for t in range(nt)]
        for k in range(g)
    ]
    scale = [None] * nt
    for j in range(g):
        tj, sj = divmod(j, 8)
        d = spread(cols[j][tj], sj)
        inv = 1.0 / d
        root = lax.rsqrt(d)
        scale[tj] = root if sj == 0 else jnp.where(sub >= sj, root, scale[tj])
        f = [None if t < tj else cols[j][t] * inv for t in range(nt)]
        for k in range(j + 1, g):
            a = spread(cols[j][k // 8], k % 8)
            for t in range(k // 8, nt):
                cols[k][t] = cols[k][t] - f[t] * a
        f[tj] = jnp.where(sub > sj, f[tj], 0.0)
        for w in range(width):
            p = spread(rows[tj][w], sj)
            for t in range(tj, nt):
                if t > tj or sj < 7:
                    rows[t][w] = rows[t][w] - f[t] * p
    return jnp.concatenate(
        [jnp.concatenate([rows[t][w] * scale[t] for w in range(width)], axis=1) for t in range(nt)], axis=0
    )


def params(mib):
    return pltpu.CompilerParams(vmem_limit_bytes=mib << 20)


def cheap(times=1):
    return pl.CostEstimate(flops=times * 3 * 10 ** 8, bytes_accessed=times * 10 ** 6, transcendentals=0)


def whole(n=1):
    return [pl.BlockSpec(memory_space=pltpu.VMEM)] * n


FAR = pl.BlockSpec(memory_space=pltpu.HBM)


def split(a):
    high = a.astype(BF16)
    return high, (a - high.astype(F32)).astype(BF16)


def dot(a, b):
    return jnp.dot(a, b, preferred_element_type=F32)


def dot3(a, b):
    return dot(a[0], b[0]) + (dot(a[0], b[1]) + dot(a[1], b[0]))


def factor_kernel(k, nb, *refs):
    earlier, (own, other, w, m) = refs[:k], refs[k:]
    core = lax.axis_index("row") % 2
    first = sum(nb - i for i in range(k))
    for j in range(nb - k):
        half, at = divmod(first + j, own.shape[0] // 128)
        rows = slice(at * 128, at * 128 + 128)
        m[:, j * 128:j * 128 + 128] = jnp.where(core == half, own[rows, :], other[rows, :])
    if k:
        m[:, (nb - k) * 128:nb * 128] = jnp.zeros((128, k * 128), F32)
    ri = lax.broadcasted_iota(jnp.int32, (128, 128), 0)
    ci = lax.broadcasted_iota(jnp.int32, (128, 128), 1)
    m[:, nb * 128:] = jnp.where(ri == ci, 1.0, 0.0)
    for i in range(k):
        at = (k - i) * 128
        known = earlier[i][:, at:]
        width = known.shape[1]
        m[:, :width] = m[:, :width] - tdot(earlier[i][:, at:at + 128], known)
    for q in range(128 // GROUP):
        lo, hi = q * GROUP, (q + 1) * GROUP
        slab = m[lo:hi, :]
        if q:
            slab = slab - tdot(w[0:lo, lo:hi], w[0:lo, :])
        w[lo:hi, :] = eliminate(slab, lo, GROUP)


def factor_rows(k, nb, earlier, packed):
    window = (nb + 1) * 128
    return pl.pallas_call(
        functools.partial(factor_kernel, k, nb),
        out_shape=jax.ShapeDtypeStruct((128, window), F32),
        in_specs=whole(k + 2),
        out_specs=whole()[0],
        scratch_shapes=[pltpu.VMEM((128, window), F32)],
        compiler_params=params(28),
        cost_estimate=cheap(),
        name="factor",
    )(*earlier, *packed)


def gather_pairs(q, step):
    out = []
    for x in range(4):
        for c in (0, 1):
            for y in range(4):
                for z in range(4):
                    flip = PAIR[(step % 2) ^ q]
                    to = (y, flip(z)) if (step // 2) ^ c == 0 else (flip(y), z)
                    out.append(((x * 2 + c) * 16 + y * 4 + z, (x * 2 + c) * 16 + to[0] * 4 + to[1]))
    return out


def gather_panel(panel):
    n = panel.shape[1] // 2
    pieces = [[panel[:, :n]], [panel[:, n:]]]
    for step in range(4):
        held = [p[0] if len(p) == 1 else jnp.concatenate(p, axis=0) for p in pieces]
        pieces = [[h, lax.ppermute(h, ("row", "col"), gather_pairs(q, step))] for q, h in enumerate(held)]
    return pieces[0] + pieces[1]


def turn_kernel(*refs):
    pieces, (o_ref, hi_ref, lo_ref) = refs[:4], refs[4:]
    order = places(lax.axis_index("row") % 2, lax.axis_index("col"))
    for i, ref in enumerate(pieces):
        q = i // 2
        for p in range(8):
            at = pl.multiple_of(order[i * 8 + p] * 64, 64)
            o_ref[pl.ds(at, 64), q * 256:q * 256 + 256] = ref[p * 64:p * 64 + 64, :]
    for j in range(0, 1024, 128):
        hi_ref[:, j:j + 128], lo_ref[:, j:j + 128] = split(jnp.transpose(o_ref[j:j + 128, :]))


def turn(pieces):
    depth, b = pieces[0].shape[0] * 2, pieces[0].shape[1] * 2
    out = jax.ShapeDtypeStruct((b, depth), BF16)
    return pl.pallas_call(
        turn_kernel,
        out_shape=(jax.ShapeDtypeStruct((depth, b), F32), out, out),
        in_specs=whole(4),
        out_specs=whole(3),
        compiler_params=params(28),
        cost_estimate=cheap(10),
        name="turn",
    )(*pieces)


def gram_kernel(p_ref, keep_ref, give_ref, blocks):
    at = 0
    for i in range(4):
        strip = tdot(p_ref[:, i * 128:i * 128 + 128], p_ref[:, i * 128:])
        for j in range(4 - i):
            blocks[at:at + 128, :] = strip[:, j * 128:j * 128 + 128]
            at += 128
    core = lax.axis_index("row") % 2
    keep_ref[...] = blocks[pl.ds(pl.multiple_of(core * 640, 128), 640), :]
    give_ref[...] = blocks[pl.ds(pl.multiple_of((1 - core) * 640, 128), 640), :]


def gram_share(rows):
    half = jax.ShapeDtypeStruct((640, 128), F32)
    return pl.pallas_call(
        gram_kernel,
        out_shape=(half, half),
        in_specs=whole(),
        out_specs=whole(2),
        scratch_shapes=[pltpu.VMEM((1280, 128), F32)],
        compiler_params=params(28),
        cost_estimate=cheap(10),
        name="gram",
    )(rows)


def swap(a, pairs):
    return lax.ppermute(a, "row", pairs)


def columns(first, i):
    return pl.ds(pl.multiple_of(first + i * TILE, TILE), TILE)


def fetch(hbm, buf, sems, first):
    def copy(i):
        return pltpu.make_async_copy(hbm.at[:, columns(first, i)], buf.at[i], sems.at[i])

    for i in range(buf.shape[0]):
        copy(i).start()
    return copy


def share_kernel(first, hi_ref, lo_ref, t_hbm, keep_ref, give_ref, buf, whole_share, sems):
    at_spot = spots(lax.axis_index("row"))
    copy = fetch(t_hbm, buf, sems, first)

    @pl.loop(0, buf.shape[0])
    def _(i):
        copy(i).wait()
        whole_share[...] = dot3((hi_ref[...], lo_ref[...]), split(buf[i]))
        for p in range(8):
            block = pl.ds(pl.multiple_of(at_spot[p] * 64, 64), 64)
            ref = (keep_ref, give_ref)[p // 4]
            ref[p % 4 * 64:p % 4 * 64 + 64, columns(0, i)] = whole_share[block, :]


def share(hi, lo, trailing, first, width):
    depth = trailing.shape[0]
    half = jax.ShapeDtypeStruct((256, width), F32)
    return pl.pallas_call(
        functools.partial(share_kernel, first),
        out_shape=(half, half),
        in_specs=whole(2) + [FAR],
        out_specs=whole(2),
        scratch_shapes=[
            pltpu.VMEM((width // TILE, depth, TILE), F32),
            pltpu.VMEM((512, TILE), F32),
            pltpu.SemaphoreType.DMA((width // TILE,)),
        ],
        compiler_params=params(28),
        cost_estimate=cheap(10),
        name="share",
    )(hi, lo, trailing)


def prepare_kernel(w0, w1, w2, w3, p_ref, r_ref, ihi_ref, ilo_ref, bhi_ref, blo_ref, inv):
    ri = lax.broadcasted_iota(jnp.int32, (128, 128), 0)
    ci = lax.broadcasted_iota(jnp.int32, (128, 128), 1)
    zero = jnp.zeros((128, 128), F32)
    for i, w in enumerate((w0, w1, w2, w3)):
        rows = slice(i * 128, i * 128 + 128)
        for j in range(4):
            cols = slice(j * 128, j * 128 + 128)
            if j < i:
                r_ref[rows, cols] = zero
            else:
                block = w[:, (j - i) * 128:(j - i) * 128 + 128]
                r_ref[rows, cols] = jnp.where(ri <= ci, block, 0.0) if j == i else block
            inv[rows, cols] = w[:, (4 - i + j) * 128:(5 - i + j) * 128] if j <= i else zero
    ihi_ref[...], ilo_ref[...] = split(inv[...])
    turned = split(jnp.transpose(inv[...]))
    for at in range(0, 1024, 256):
        rows = slice(at, at + 256)
        bhi_ref[rows, :], blo_ref[rows, :] = split(dot3(split(p_ref[rows, :]), turned))


def prepare(factors, rows):
    b = rows.shape[1]
    square, tall = (b, b), rows.shape
    return pl.pallas_call(
        prepare_kernel,
        out_shape=[jax.ShapeDtypeStruct(s, t) for s, t in ((square, F32), (square, BF16), (square, BF16), (tall, BF16), (tall, BF16))],
        in_specs=whole(5),
        out_specs=whole(5),
        scratch_shapes=[pltpu.VMEM(square, F32)],
        compiler_params=params(28),
        cost_estimate=cheap(),
        name="prepare",
    )(*factors, rows)


def finish_kernel(first, *refs):
    pieces, (ihi, ilo, bhi, blo, t_hbm) = refs[:4], refs[4:9]
    c_hbm, o_hbm, buf, total, cbuf, in_sems, c_sems, o_sems = refs[-8:]
    n = total.shape[0] // 2
    at_spot = spots(lax.axis_index("row"))
    copy = fetch(t_hbm, buf, in_sems, first)
    tall = buf.shape[1] // 2

    def c_copy(i):
        return pltpu.make_async_copy(cbuf.at[i], c_hbm.at[:, columns(first, i)], c_sems.at[i])

    def o_copy(i, r):
        rows = pl.ds(pl.multiple_of(r * tall, tall), tall)
        return pltpu.make_async_copy(buf.at[i, rows, :], o_hbm.at[rows, columns(first, i)], o_sems.at[2 * i + r])

    @pl.loop(0, buf.shape[0])
    def _(i):
        for p in range(8):
            at = pl.multiple_of(at_spot[p] * 64, 64)
            total[pl.ds(at, 64), :] = pieces[p // 2][p % 2 * 64:p % 2 * 64 + 64, columns(0, i)]
        high, low = split(total[...])
        for rows, depth in ((slice(0, n), n), (slice(n, 2 * n), 2 * n)):
            cbuf[i, rows, :] = dot3((ihi[rows, :depth], ilo[rows, :depth]), (high[:depth, :], low[:depth, :]))
        c_copy(i).start()
        c = split(cbuf[i])
        copy(i).wait()

        @pl.loop(0, 2)
        def _(r):
            rows = pl.ds(pl.multiple_of(r * tall, tall), tall)
            buf[i, rows, :] = buf[i, rows, :] - dot3((bhi[rows, :], blo[rows, :]), c)
            o_copy(i, r).start()

    @pl.loop(0, buf.shape[0])
    def _(i):
        c_copy(i).wait()
        o_copy(i, 0).wait()
        o_copy(i, 1).wait()


def finish(pieces, ihi, ilo, bhi, blo, trailing, first, done):
    depth, width = trailing.shape
    b = ihi.shape[0]
    tiles = pieces[0].shape[1] // TILE
    return pl.pallas_call(
        functools.partial(finish_kernel, first),
        out_shape=(jax.ShapeDtypeStruct((b, width), F32), jax.ShapeDtypeStruct((depth, width), F32)),
        in_specs=whole(8) + [FAR] * (1 + len(done)),
        out_specs=(FAR, FAR),
        scratch_shapes=[
            pltpu.VMEM((tiles, depth, TILE), F32),
            pltpu.VMEM((b, TILE), F32),
            pltpu.VMEM((tiles, b, TILE), F32),
            pltpu.SemaphoreType.DMA((tiles,)),
            pltpu.SemaphoreType.DMA((tiles,)),
            pltpu.SemaphoreType.DMA((2 * tiles,)),
        ],
        input_output_aliases={9 + i: i for i in range(len(done))},
        compiler_params=params(28),
        cost_estimate=cheap(),
        name="finish",
    )(*pieces, ihi, ilo, bhi, blo, trailing, *done)


def after(value, *others):
    return lax.optimization_barrier((value, others))[0]


def local(panel, trailing):
    rows, hi, lo = turn(gather_panel(panel))
    width = trailing.shape[1] // 2
    gram_keep, gram_give = gram_share(rows)
    gram_came = swap(gram_give, CORE)
    gram = gram_keep + gram_came
    came = swap(gram, ROW[0])
    first = share(after(hi, gram), lo, trailing, 0, width)
    gram = after(gram, first[0]) + came
    came = swap(gram, ROW[1])
    second = share(after(hi, gram, first[0]), lo, trailing, width, width)
    gram = gram + came
    second, gram = lax.optimization_barrier((second, gram))

    keeps, gives = [], []
    for keep, give in (first, second):
        got = swap(give, CORE)
        gives.append(keep[128:] + got[128:])
        keeps.append(keep[:128] + got[:128])
    came = [swap(g, ROW[0]) for g in gives]
    packed = (gram, swap(gram, CORE))
    factors = []
    for c in (0, 1):
        factors.append(factor_rows(c, 4, factors, packed))
        came[c], keeps[c], factors[-1] = lax.optimization_barrier((came[c], keeps[c], factors[-1]))
        give, keeps[c] = keeps[c][64:] + came[c][64:], keeps[c][:64] + came[c][:64]
        came[c] = swap(give, ROW[1])
    own = []
    for c in (0, 1):
        factors.append(factor_rows(2 + c, 4, factors, packed))
        came[c], keeps[c], factors[-1] = lax.optimization_barrier((came[c], keeps[c], factors[-1]))
        own.append(keeps[c] + came[c])
        came[c] = swap(own[c], ROW[1])
    own = [jnp.concatenate(p, axis=0) for p in zip(own, came)]
    r_factor, ihi, ilo, bhi, blo = prepare(factors, after(rows, own[0]))
    came = [swap(own[0], ROW[0])]
    came[0], ihi = lax.optimization_barrier((came[0], ihi))
    own[1] = after(own[1], came[0])
    came.append(swap(own[1], ROW[0]))
    own_across = [swap(p, CORE) for p in own]
    done = ()
    for c in (0, 1):
        pieces = [own[c], came[c], own_across[c], swap(came[c], CORE)]
        done = finish(pieces, ihi, ilo, bhi, blo, trailing, c * width, done)
        if c == 0:
            done, came = lax.optimization_barrier((done, came))
    return (r_factor, *done)


def solution(mesh):
    placed = (P(("row", "col"), None), P("row", "col"))
    return jax.shard_map(
        local,
        mesh=mesh,
        in_specs=placed,
        out_specs=(P(), P(None, "col"), P("row", "col")),
        check_vma=False,
    )
```
